128 devices in a mesh: dp: 8 (over x, core), ep: 16 (over z, y).
Axes of the slice: x: 4, y: 4, z: 4, core: 2. Of those that a mesh axis runs over, the one named last changes fastest.
Arguments:
- hidden: bfloat16 [256, 7168], P(('dp', 'ep')), may hold values from -20 to 20
- q_latent: bfloat16 [256, 64, 512], P(('dp', 'ep')), may hold values from -48 to 48
- q_rope: bfloat16 [256, 64, 64], P(('dp', 'ep')), may hold values from -48 to 48
- latent_pages: bfloat16 [3072, 64, 512], P(('dp', 'ep')), may hold values from -8 to 8
- rope_pages: bfloat16 [3072, 32, 128], P(('dp', 'ep')), may hold values from -8 to 8
- block_table: int32 [256, 12], P(('dp', 'ep')), may hold values from 0 to 23, as said below
- cache_len: int32 [256], P(('dp', 'ep')), may hold values from 2 to 768, as said below
- move_req: int32 [128], P(('dp', 'ep')), may hold values from 0 to 1, as said below
- move_to: int32 [128], P(('dp', 'ep')), may hold values from 0 to 7, as said below
- routing: int32 [256, 8], P(('dp', 'ep')), may hold values from 0 to 15, all different within a row; in each aligned block of 2 rows (0 to 1, 2 to 3, ...) at most 2 rows name the same one
- gate_weight: float32 [256, 8], P(('dp', 'ep')), may hold values from 0.1 to 1
- norm_gain: float32 [7168], replicated, may hold values from 0.1 to 1.9
- w_uv: bfloat16 [64, 512, 128], P('ep'), may hold values from -0.25 to 0.25
- w_out: bfloat16 [8192, 7168], P('ep'), may hold values from -0.5 to 0.5
- w_gate: bfloat16 [16, 7168, 2048], P('ep', None, 'dp'), may hold values from -0.0625 to 0.0625
- w_up: bfloat16 [16, 7168, 2048], P('ep', None, 'dp'), may hold values from -0.0625 to 0.0625
- w_down: bfloat16 [16, 2048, 7168], P('ep', 'dp'), may hold values from -0.125 to 0.125
Outputs:
- mixed: bfloat16 [256, 7168], P(('dp', 'ep'))
The draws below stay inside these ranges and needn't reach their ends.
Inputs may be any that keep to these rules, and one draw needn't show every extreme that they name: `block_table`: each row names pages of its home device's own block of 24 pages by their index within that block; no page is named twice. `cache_len`: every handed-off request has exactly 768 cache positions. `move_req`: every device hands off exactly one request. `move_to`: among the devices of one ep index these dp indices form a permutation: each device hands off one request and receives one; a device may keep its own. `routing`: rows in the new layout. Each row names 8 different experts; among the rows of one device no expert is named more than 2 times, and some device reaches it.
All inputs are finite; a program needn't handle non-finite values.
Results may differ from the reference program's by a relative error of at most 0.023.
Values may be sent and summed in bfloat16 or wider, within the bound.
A program may use at most 128 MiB of HBM per device.

```python
import math
import jax
import jax.numpy as jnp
import numpy as np
from jax import lax

D = 7168
HEADS = 64
LAT = 512
ROPE = 64
VDIM = 128
EXP_FF = 2048
TOPK = 8
PAGE = 64
R_DEV = 2
MAXP = 12
POOL = 24
EXPERTS = 16
CAP = 2
REQS = 256
N_DP = 8
N_EP = 16
DEVICES = 128


def page_order(key):
    sub = jax.random.fold_in(key, 501)
    streams = jax.random.split(sub, DEVICES)
    orders = jax.vmap(lambda stream: jax.random.permutation(stream, R_DEV * MAXP))(streams)
    return orders.reshape(DEVICES * R_DEV, MAXP).astype(jnp.int32)


def page_values(key):
    sub = jax.random.fold_in(key, 502)
    first, second = jax.random.split(sub)
    latent = jnp.clip(jax.random.normal(first, (DEVICES * R_DEV * MAXP, PAGE, LAT), jnp.float32), -6.0, 6.0)
    rotary = jnp.clip(jax.random.normal(second, (DEVICES * R_DEV * MAXP, PAGE, ROPE), jnp.float32), -6.0, 6.0)
    latent = latent.at[:, 1].set(latent[:, 1])
    rotary = rotary.at[:, 1].set(rotary[:, 1])
    return (latent, rotary)


def hand_offs(key):
    sub = jax.random.fold_in(key, 504)
    first, second = jax.random.split(sub)
    slots = jax.random.randint(first, (N_DP, N_EP), 0, R_DEV)
    targets = jax.vmap(lambda stream: jax.random.permutation(stream, N_DP))(jax.random.split(second, N_EP)).astype(jnp.int32)
    return (slots.reshape(DEVICES).astype(jnp.int32), targets.T.reshape(DEVICES).astype(jnp.int32))


def draw_hidden(key, part):
    own = jax.random.fold_in(key, 11)
    first = jax.random.fold_in(own, 0)
    values = jnp.clip(jax.random.normal(first, (DEVICES * R_DEV, D), jnp.float32), -6.0, 6.0)
    return values.astype(jnp.bfloat16)


def draw_q_latent(key, part):
    own = jax.random.fold_in(key, 12)
    values = jnp.clip(jax.random.normal(own, (DEVICES * R_DEV, HEADS, LAT), jnp.float32), -6.0, 6.0)
    return values.astype(jnp.bfloat16)


def draw_q_rope(key, part):
    own = jax.random.fold_in(key, 13)
    values = jnp.clip(jax.random.normal(own, (DEVICES * R_DEV, HEADS, ROPE), jnp.float32), -6.0, 6.0)
    return values.astype(jnp.bfloat16)


def draw_latent_pages(key, part):
    latent, rotary = page_values(key)
    return latent.astype(jnp.bfloat16)


def draw_rope_pages(key, part):
    latent, rotary = page_values(key)
    return rotary.reshape(DEVICES * R_DEV * MAXP, PAGE // 2, 2 * ROPE).astype(jnp.bfloat16)


def draw_block_table(key, part):
    return page_order(key)


def draw_cache_len(key, part):
    own = jax.random.fold_in(key, 17)
    lengths = jax.random.randint(own, (DEVICES, R_DEV), 2, MAXP * PAGE + 1)
    slots, targets = hand_offs(key)
    lengths = jnp.where(jnp.arange(R_DEV)[None, :] == slots[:, None], MAXP * PAGE, lengths)
    return lengths.reshape(DEVICES * R_DEV).astype(jnp.int32)


def draw_move_req(key, part):
    slots, targets = hand_offs(key)
    return slots


def draw_move_to(key, part):
    slots, targets = hand_offs(key)
    return targets


def shard_levels(own_key, dims, shards, least, high):
    def one(position, blocks):
        draws = jax.random.uniform(jax.random.fold_in(jax.random.fold_in(own_key, 6), position), (blocks,), jnp.float32, least / len(shards), high / len(shards))
        return jnp.repeat(jnp.exp(draws), dims[position] // blocks).reshape((-1,) + (1,) * (len(dims) - position - 1))

    gain = one(*shards[0])
    for cut in shards[1:]:
        gain = gain * one(*cut)
    return gain


def deal_out(rng, own, number, rows, count, top, limit, slope):
    order = jax.random.permutation(rng, count)
    crowded, common = shares(count, rows * top, limit, slope, True), shares(count, rows * top, limit, slope, False)
    places = jnp.arange(count)

    def named(tallies, rotation):
        used = int((tallies > 0).sum())
        fixed = max(1, used // 4)
        moved = fixed + (places - fixed + rotation * (used - fixed)) % max(1, count - fixed)
        return jnp.zeros((count,), jnp.int32).at[order[jnp.where(places < fixed, places, moved)]].set(jnp.asarray(tallies, jnp.int32))

    tallies = jnp.where(number % 4 == 0, named(crowded, number // 4), named(common, number - number // 4 - 1))
    mixed = jax.random.permutation(jax.random.fold_in(own, 3), count)
    source_of, sink = mixed[0:count // 2 * 2:2], mixed[1:count // 2 * 2:2]
    slack = jnp.minimum(tallies[source_of] - 1, limit - tallies[sink]) // 2
    slack = jnp.where((source_of == order[0]) | (sink == order[0]) | (tallies[sink] == 0), 0, jnp.maximum(slack, 0))
    moved = jax.random.randint(jax.random.fold_in(own, 4), (count // 2,), 0, 1 << 20) % (slack + 1)
    tallies = tallies.at[source_of].add(-moved).at[sink].add(moved)
    members = jnp.searchsorted(jnp.cumsum(tallies), jnp.arange(rows * top), side="right").astype(jnp.int32)
    listing = members.reshape(top, rows).T
    listing = listing[jax.random.permutation(jax.random.fold_in(own, 1), rows)]
    rotation = jax.random.randint(jax.random.fold_in(own, 2), (rows, 1), 0, top)
    return jnp.take_along_axis(listing, (jnp.arange(top)[None, :] + rotation) % top, axis=1)


def shares(number_of, total, bound, lean, full):
    portions = [(1 << 20) // math.isqrt(grade ** lean) + 1 for grade in range(1, number_of + 1)]
    largest = bound if full else min(bound, max(-(-total // number_of), total * portions[0] // sum(portions)))
    least = 1 if total - largest >= number_of - 1 else 0
    given, surplus = [largest] + [least] * (number_of - 1), total - largest - least * (number_of - 1)
    while surplus > 0:
        free = [i for i in range(1, number_of) if given[i] < largest] or [i for i in range(1, number_of) if given[i] < bound]
        pool, budget = sum([portions[i] for i in free]), surplus
        for i in free:
            addition = min(bound - given[i], max(1, budget * portions[i] // pool), surplus)
            given[i] = given[i] + addition
            surplus = surplus - addition
    return np.array(given)


def bell_draw(rng, shape, deviation, bound, cuts=(), held_as=jnp.bfloat16):
    drawn = deviation * jax.random.normal(rng, shape, jnp.float32)
    if cuts:
        drawn = drawn * shard_levels(rng, shape, cuts, -0.22, 0.18)
    return jnp.clip(drawn, -bound, bound).astype(held_as)


def setup_inputs(seed: int = 0) -> dict:
    seeds = jax.random.split(jax.random.key(seed), 18)
    hidden = draw_hidden(jax.random.fold_in(seeds[17], 71), 0)
    q_latent = draw_q_latent(jax.random.fold_in(seeds[17], 71), 0)
    q_rope = draw_q_rope(jax.random.fold_in(seeds[17], 71), 0)
    latent_pages = draw_latent_pages(jax.random.fold_in(seeds[17], 71), 0)
    rope_pages = draw_rope_pages(jax.random.fold_in(seeds[17], 71), 0)
    block_table = draw_block_table(jax.random.fold_in(seeds[17], 71), 0)
    cache_len = draw_cache_len(jax.random.fold_in(seeds[17], 71), 0)
    move_req = draw_move_req(jax.random.fold_in(seeds[17], 71), 0)
    move_to = draw_move_to(jax.random.fold_in(seeds[17], 71), 0)
    routing_keys = jax.random.split(jax.random.fold_in(seeds[9], 1), REQS // R_DEV)
    routing_turns = jax.random.permutation(jax.random.fold_in(seeds[9], 3), REQS // R_DEV)
    routing = jax.vmap(lambda own, number: deal_out(jax.random.fold_in(seeds[9], 2), own, number, R_DEV, EXPERTS, TOPK, CAP, 1))(routing_keys, routing_turns).reshape((REQS, TOPK))
    gate_weight = jnp.clip(jnp.exp(math.log(1.0) - 2.3025851 * jax.random.uniform(seeds[10], (REQS, TOPK), jnp.float32) ** shard_levels(seeds[10], (REQS, TOPK), ((0, 128),), -0.2, 0.2)), 0.1, 1.0)
    norm_gain = jnp.clip(1.0 + 0.18 * jax.random.normal(seeds[11], (D,), jnp.float32), 0.1, 1.9)
    w_uv = bell_draw(seeds[12], (HEADS, LAT, VDIM), LAT ** -0.5, 0.25, ((0, 16),))
    w_out = bell_draw(seeds[13], (HEADS * VDIM, D), VDIM ** -0.5, 0.5, ((0, 16),))
    w_gate = bell_draw(seeds[14], (EXPERTS, D, EXP_FF), D ** -0.5, 0.0625, ((0, 16), (2, 8)))
    w_up = bell_draw(seeds[15], (EXPERTS, D, EXP_FF), D ** -0.5, 0.0625, ((0, 16), (2, 8)))
    w_down = bell_draw(seeds[16], (EXPERTS, EXP_FF, D), EXP_FF ** -0.5, 0.125, ((0, 16), (1, 8)))
    return {"hidden": hidden, "q_latent": q_latent, "q_rope": q_rope, "latent_pages": latent_pages, "rope_pages": rope_pages, "block_table": block_table, "cache_len": cache_len, "move_req": move_req, "move_to": move_to, "routing": routing, "gate_weight": gate_weight, "norm_gain": norm_gain, "w_uv": w_uv, "w_out": w_out, "w_gate": w_gate, "w_up": w_up, "w_down": w_down}


def reference(hidden, q_latent, q_rope, latent_pages, rope_pages, block_table, cache_len, move_req, move_to, routing, gate_weight, norm_gain, w_uv, w_out, w_gate, w_up, w_down):
    scale = (VDIM + ROPE) ** (-0.5)
    home = (jnp.arange(REQS) // R_DEV).astype(jnp.int32)
    global_pages = (block_table + (home * POOL)[:, None]).astype(jnp.int32)
    rope_table = rope_pages.reshape(DEVICES * POOL, PAGE, ROPE)
    places = jnp.arange(MAXP * PAGE)

    def attend(inputs):
        query_row, rotary_row, page_rows, length = inputs
        latent_keys = latent_pages[page_rows].reshape(MAXP * PAGE, LAT)
        rotary_keys = rope_table[page_rows].reshape(MAXP * PAGE, ROPE)
        scores = jnp.dot(query_row, latent_keys.T, preferred_element_type=jnp.float32)
        scores = (scores + jnp.dot(rotary_row, rotary_keys.T, preferred_element_type=jnp.float32)) * scale
        scores = jnp.where(places[None, :] < length, scores, -jnp.inf)
        largest = lax.optimization_barrier(jnp.max(scores, axis=1, keepdims=True))
        weights = jnp.exp(scores - largest)
        totals = lax.optimization_barrier(jnp.sum(weights, axis=1, keepdims=True))
        gathered = jnp.dot(weights.astype(jnp.bfloat16), latent_keys, preferred_element_type=jnp.float32)
        return (gathered / totals).astype(jnp.bfloat16)
    latent_out = lax.map(attend, (q_latent, q_rope, global_pages, cache_len))
    values = jnp.einsum('rhl,hlv->rhv', latent_out.astype(jnp.float32), w_uv.astype(jnp.float32)).astype(jnp.bfloat16)
    attention = jnp.dot(values.reshape(REQS, HEADS * VDIM), w_out, preferred_element_type=jnp.float32)
    attended = (hidden.astype(jnp.float32) + attention).astype(jnp.bfloat16)
    devices_all = jnp.arange(DEVICES, dtype=jnp.int32)
    target_device = (move_to * N_EP + devices_all % N_EP).astype(jnp.int32)
    source_rows = (devices_all * R_DEV + move_req).astype(jnp.int32)
    target_rows = (target_device * R_DEV + move_req[target_device]).astype(jnp.int32)
    moved = attended.at[target_rows].set(attended[source_rows])
    widened = moved.astype(jnp.float32)
    mean_square = lax.optimization_barrier(jnp.mean(widened * widened, axis=1, keepdims=True))
    normed = (widened * lax.rsqrt(mean_square + 1e-06) * norm_gain).astype(jnp.bfloat16)
    onehot = (routing[:, :, None] == jnp.arange(EXPERTS, dtype=jnp.int32)[None, None, :]).astype(jnp.int32)
    named = lax.optimization_barrier(jnp.sum(onehot, axis=1)).reshape(DEVICES, R_DEV, EXPERTS)
    slot_rank = (jnp.cumsum(named, axis=1) - named).reshape(REQS, EXPERTS)
    token_rank = lax.optimization_barrier(jnp.sum(onehot * slot_rank[:, None, :], axis=2))
    device_of = (jnp.arange(REQS) // R_DEV).astype(jnp.int32)
    slot_index = (routing * (DEVICES * CAP) + device_of[:, None] * CAP + token_rank).astype(jnp.int32)
    total_slots = EXPERTS * DEVICES * CAP
    holder = jnp.zeros((total_slots,), jnp.int32).at[slot_index.reshape(-1)].set(jnp.repeat(jnp.arange(REQS, dtype=jnp.int32), TOPK))
    filled = jnp.zeros((total_slots,), jnp.bool_).at[slot_index.reshape(-1)].set(True)
    expert_in = jnp.where(filled[:, None], normed[holder], jnp.zeros((), jnp.bfloat16))
    expert_in = expert_in.reshape(EXPERTS, DEVICES * CAP, D)
    block_width = EXP_FF // N_DP

    def expert(inputs):
        rows_in, gate_proj, up_proj, down_proj = inputs
        gated = jnp.dot(rows_in, gate_proj, preferred_element_type=jnp.float32)
        upward = jnp.dot(rows_in, up_proj, preferred_element_type=jnp.float32)
        inner = (jax.nn.silu(gated) * upward).astype(jnp.bfloat16)
        pieces = jnp.einsum('rcf,cfd->crd', inner.reshape(DEVICES * CAP, N_DP, block_width).astype(jnp.float32), down_proj.reshape(N_DP, block_width, D).astype(jnp.float32))
        pieces = lax.optimization_barrier(pieces.astype(jnp.bfloat16)).astype(jnp.float32)
        return lax.optimization_barrier(jnp.sum(pieces, axis=0)).astype(jnp.bfloat16)
    expert_out = lax.map(expert, (expert_in, w_gate, w_up, w_down))
    flat_out = expert_out.reshape(total_slots, D)
    routed = jnp.zeros((REQS, D), jnp.float32)
    for top_index in range(TOPK):
        routed = routed + gate_weight[:, top_index, None] * flat_out[slot_index[:, top_index]].astype(jnp.float32)
    return (widened + routed).astype(jnp.bfloat16)
```

```python
import functools

import jax
import jax.numpy as jnp
from jax import lax
from jax.experimental import pallas as pl
from jax.experimental.pallas import tpu as pltpu
from jax.sharding import PartitionSpec as P

MESH = pl.DeviceIdType.MESH
BF = jnp.bfloat16
F32 = jnp.float32

D = 7168
HALF = D // 2
BLK = 896
PIECES = (384, 256, 256)
STARTS = (0, 384, 640)
GATHER = (("y", "z", "x"), ("z", "x", "y"), ("x", "y", "z"))
REDUCE = (("x", "y", "z"), ("y", "z", "x"), ("z", "x", "y"))
BASE = (0, 5, 10)
COUNT = (5, 5, 4)
CHUNKS = [(p, q) for q in range(5) for p in range(3) if q < COUNT[p]]

SCRATCH = dict(
    qv=pltpu.VMEM((2, 64, 512), BF),
    qrv=pltpu.VMEM((2, 64, 64), BF),
    pgv=pltpu.VMEM((24, 64, 512), BF),
    rpv=pltpu.VMEM((24, 32, 128), BF),
    uvv=pltpu.VMEM((4, 512, 128), BF),
    wov=pltpu.VMEM((8, 512, BLK), BF),
    wv=pltpu.VMEM((4, HALF, 256), BF),
    wd=pltpu.VMEM((2, 256, HALF), BF),
    scores=pltpu.VMEM((6, 128, 256), F32),
    a_send=pltpu.VMEM((16, 16, 256), BF),
    a_recv=pltpu.VMEM((16, 16, 256), BF),
    r_send=pltpu.VMEM((8, 2, 16, BLK), BF),
    r_recv=pltpu.VMEM((16, 16, BLK), BF),
    m_one=pltpu.VMEM((16, 8, 128), F32),
    m_all=pltpu.VMEM((8, 16, 128), F32),
    xa=pltpu.VMEM((4, 4, 4, 16, PIECES[0]), BF),
    xb=pltpu.VMEM((4, 4, 4, 16, PIECES[1]), BF),
    xc=pltpu.VMEM((4, 4, 4, 16, PIECES[2]), BF),
    xg=pltpu.VMEM((256, BLK), BF),
    pre=pltpu.VMEM((4, 256, 256), F32),
    squares=pltpu.VMEM((256, 128), F32),
    squares_in=pltpu.VMEM((256, 128), F32),
    pre_send=pltpu.VMEM((4, 256, 256), BF),
    pre_recv=pltpu.VMEM((4, 256, 256), BF),
    inner=pltpu.VMEM((2, 256, 256), BF),
    sorted_in=pltpu.VMEM((3, 2, 256, 256), BF),
    perm=pltpu.VMEM((3, 256, 256), BF),
    weight=pltpu.VMEM((3, 256, 128), F32),
    resid=pltpu.VMEM((16, HALF), F32),
    c_send=pltpu.VMEM((14, 4, 64, 256), BF),
    c_recv=pltpu.VMEM((14, 4, 64, 256), BF),
    b_send=pltpu.VMEM((14, 4, 16, 256), BF),
    b_recv=pltpu.VMEM((14, 4, 16, 256), BF),
    f_send=pltpu.VMEM((3, 8, 2, 1280), F32),
    f_recv=pltpu.VMEM((3, 8, 2, 1280), F32),
    load_sem=pltpu.SemaphoreType.DMA((16,)),
    swap_s=pltpu.SemaphoreType.DMA((8,)),
    swap_r=pltpu.SemaphoreType.DMA((8,)),
    a_s=pltpu.SemaphoreType.DMA((16,)),
    a_r=pltpu.SemaphoreType.DMA((16,)),
    r_s=pltpu.SemaphoreType.DMA((16,)),
    r_r=pltpu.SemaphoreType.DMA((16,)),
    m_s=pltpu.SemaphoreType.DMA((16,)),
    m_r=pltpu.SemaphoreType.DMA((16,)),
    n_s=pltpu.SemaphoreType.DMA((8,)),
    n_r=pltpu.SemaphoreType.DMA((8,)),
    g_s=pltpu.SemaphoreType.DMA((2, 3, 4)),
    g_r=pltpu.SemaphoreType.DMA((2, 3, 4)),
    h_s=pltpu.SemaphoreType.DMA((3, 4, 4)),
    h_r=pltpu.SemaphoreType.DMA((3, 4, 4)),
    c_s=pltpu.SemaphoreType.DMA((14, 4)),
    c_r=pltpu.SemaphoreType.DMA((14, 4)),
    b_s=pltpu.SemaphoreType.DMA((14, 4)),
    b_r=pltpu.SemaphoreType.DMA((14, 4)),
    f_s=pltpu.SemaphoreType.DMA((3, 8)),
    f_r=pltpu.SemaphoreType.DMA((3, 8)),
)


def iota(shape, dim):
    return lax.broadcasted_iota(jnp.int32, shape, dim)


def ones_where(mask):
    return jnp.where(mask, 1.0, 0.0).astype(BF)


def dot(a, b):
    return jnp.dot(a, b, preferred_element_type=F32)


def dot_nt(a, b):
    return lax.dot_general(a, b, (((1,), (1,)), ((), ())), preferred_element_type=F32)


def layer(
    hidden,
    gain,
    table,
    lens,
    move_req,
    move_to,
    routing,
    gates,
    q_latent,
    q_rope,
    pages,
    ropes,
    w_uv,
    w_out,
    w_gate,
    w_up,
    w_down,
    out,
    *scratch,
):
    s = dict(zip(SCRATCH, scratch))
    i = lax.axis_index("dp")
    j = lax.axis_index("ep")
    x, c = lax.div(i, 2), lax.rem(i, 2)
    z, y = lax.div(j, 4), lax.rem(j, 4)
    other = 1 - c
    at = {"x": x, "y": y, "z": z}

    def place(axis, value, core):
        if axis == "x":
            return (value * 2 + core, j)
        if axis == "y":
            return (x * 2 + core, z * 4 + value)
        return (x * 2 + core, value * 4 + y)

    def turn(axis, k):
        return lax.rem(at[axis] + k, 4)

    def remote(src, dst, send, recv, device):
        return pltpu.make_async_remote_copy(
            src_ref=src, dst_ref=dst, send_sem=send, recv_sem=recv, device_id=device, device_id_type=MESH
        )

    sibling = (x * 2 + other, j)

    barrier = pltpu.get_barrier_semaphore()

    def greet(m, carry):
        t = lax.rem(c * 16 + j + m, 32)
        pl.semaphore_signal(
            barrier, inc=1, device_id=(x * 2 + lax.div(t, 16), lax.rem(t, 16)), device_id_type=MESH
        )
        return carry

    lax.fori_loop(1, 32, greet, 0)
    for k in (1, 2, 3):
        for core in (0, 1):
            pl.semaphore_signal(barrier, inc=1, device_id=place("x", turn("x", k), core), device_id_type=MESH)

    half = pl.multiple_of(c * HALF, 128)
    others = pl.multiple_of(other * HALF, 128)
    loads = [
        (q_latent, s["qv"]),
        (q_rope, s["qrv"]),
        (ropes, s["rpv"]),
        (pages, s["pgv"]),
        (w_uv, s["uvv"]),
    ]
    loads += [(w_out.at[:, pl.ds(n * BLK, BLK)], s["wov"].at[n]) for n in range(8)]
    loads += [
        (w_gate.at[0, pl.ds(half, HALF), :], s["wv"].at[0]),
        (w_up.at[0, pl.ds(half, HALF), :], s["wv"].at[1]),
        (w_down.at[0, :, pl.ds(half, HALF)], s["wd"].at[0]),
    ]
    loads = [pltpu.make_async_copy(src, dst, s["load_sem"].at[n]) for n, (src, dst) in enumerate(loads)]
    for load in loads:
        load.start()

    row = iota((128, 128), 0)
    col = iota((128, 128), 1)
    wanted = lax.rem(lax.div(row, 4), 2) * 64 + lax.div(row, 8) * 4 + lax.rem(row, 4)
    order = ones_where(col == wanted)
    twice = ones_where(iota((64, 128), 0) == lax.rem(iota((64, 128), 1), 64))
    first_row = lax.rem(lax.div(iota((128, 1), 0), 4), 2) == 0
    spread = ones_where(lax.div(iota((256, 128), 0), 2) == iota((256, 128), 1))
    parity = lax.div(iota((256, 128), 1), 64) == lax.rem(iota((256, 128), 0), 2)
    place_of = iota((1, 1536), 1)
    bias = []
    for r in range(2):
        live = jnp.zeros((1, 1536), jnp.int32)
        for q in range(12):
            start = table[r, q] * 64
            count = jnp.clip(lens[r] - q * 64, 0, 64)
            live = jnp.where((place_of >= start) & (place_of < start + count), 1, live)
        bias.append(jnp.where(live > 0, 0.0, -1e30))
    scale = 192.0 ** (-0.5)
    loads[0].wait()
    loads[1].wait()
    query = dot(order, s["qv"][...].reshape(128, 512)).astype(BF)
    rotary = dot(dot(order, s["qrv"][...].reshape(128, 64)).astype(BF), twice).astype(BF)
    loads[2].wait()
    loads[3].wait()
    largest = jnp.full((128, 1), -1e30, F32)
    for n in range(6):
        keys = s["pgv"][4 * n : 4 * n + 4].reshape(256, 512)
        turned = dot(spread, s["rpv"][4 * n : 4 * n + 4].reshape(128, 128))
        turned = jnp.where(parity, turned, 0.0).astype(BF)
        score = (dot_nt(query, keys) + dot_nt(rotary, turned)) * scale
        cut = slice(256 * n, 256 * n + 256)
        score = score + jnp.where(first_row, bias[0][:, cut], bias[1][:, cut])
        s["scores"][n] = score
        largest = jnp.maximum(largest, jnp.max(score, axis=1, keepdims=True))
    total = jnp.zeros((128, 1), F32)
    mixed = jnp.zeros((128, 512), F32)
    for n in range(6):
        prob = jnp.exp(s["scores"][n] - largest)
        total = total + jnp.sum(prob, axis=1, keepdims=True)
        mixed = mixed + dot(prob.astype(BF), s["pgv"][4 * n : 4 * n + 4].reshape(256, 512))
    mixed = mixed / total
    lower = mixed[:, :256].reshape(16, 8, 256)
    upper = mixed[:, 256:].reshape(16, 8, 256)
    s["a_send"][...] = jnp.concatenate([lower, upper], axis=1).astype(BF)
    s["a_recv"][j] = s["a_send"][j]

    pl.semaphore_wait(barrier, 37)

    def a_copy(k, land):
        t = lax.rem(j + k, 16)
        return remote(s["a_send"].at[t], s["a_recv"].at[land], s["a_s"].at[k], s["a_r"].at[k], (i, t))

    def a_start(k, carry):
        a_copy(k, j).start()
        return carry

    lax.fori_loop(1, 16, a_start, 0)

    lane = iota((8, 128), 1)
    note = jnp.zeros((8, 128), F32)
    for r in range(2):
        for k in range(8):
            note = jnp.where(lane == routing[r, k] + 16 * r, gates[r, k], note)
    note = jnp.where(lane == 32, move_req[0].astype(F32), note)
    note = jnp.where(lane == 33, move_to[0].astype(F32), note)
    s["m_one"][j] = jnp.where(iota((8, 128), 0) == 0, note, 0.0)

    def m_copy(k, land):
        t = lax.rem(j + k, 16)
        return remote(s["m_one"].at[land], s["m_one"].at[land], s["m_s"].at[k], s["m_r"].at[k], (i, t))

    def m_start(k, carry):
        m_copy(k, j).start()
        return carry

    lax.fori_loop(1, 16, m_start, 0)

    swaps = [
        (w_gate.at[0, pl.ds(others, HALF), :], s["wv"].at[2]),
        (w_up.at[0, pl.ds(others, HALF), :], s["wv"].at[3]),
        (w_down.at[0, :, pl.ds(others, HALF)], s["wd"].at[1]),
    ]
    swaps = [remote(a, b, s["swap_s"].at[n], s["swap_r"].at[n], sibling) for n, (a, b) in enumerate(swaps)]
    for swap in swaps:
        swap.start()

    def a_wait(k, carry):
        a_copy(k, lax.rem(j + 16 - k, 16)).wait_recv()
        return carry

    target = iota((256, 256), 0)
    inside = lax.rem(target, 128)
    wanted = (
        lax.div(lax.rem(inside, 32), 2) * 16
        + lax.div(target, 128) * 8
        + lax.rem(inside, 2) * 4
        + lax.div(inside, 32)
    )
    by_head = ones_where(iota((256, 256), 1) == wanted)
    loads[4].wait()
    lax.fori_loop(1, 16, a_wait, 0)
    grouped = dot(by_head, s["a_recv"][...].reshape(256, 256)).astype(BF)
    values = []
    for h in range(4):
        low = grouped[32 * h : 32 * h + 32]
        high = grouped[128 + 32 * h : 160 + 32 * h]
        values.append((dot(low, s["uvv"][h, :256]) + dot(high, s["uvv"][h, 256:])).astype(BF))
    values = jnp.concatenate(values, axis=1)
    for n in range(8):
        loads[5 + n].wait()
    request = iota((32, 1), 0)

    def r_target(n, h):
        core, zz = lax.div(n, 4), lax.rem(n, 4)
        return core, zz, 2 * c + h

    def r_copy(n, h):
        core, zz, yy = r_target(n, h)
        m = n * 2 + h
        return remote(
            s["r_send"].at[n, h],
            s["r_recv"].at[j],
            s["r_s"].at[m],
            s["r_r"].at[j],
            (x * 2 + core, zz * 4 + yy),
        )

    def r_mine(n, h):
        core, zz, yy = r_target(n, h)
        return (core == c) & (zz == z) & (yy == y)

    def r_start(n, carry):
        width = pl.multiple_of(n * BLK, 128)
        part = dot(values, s["wov"][n])
        own = hidden[:, pl.ds(width, BLK)].astype(F32)
        part = part + jnp.where(
            request == 2 * j, own[0:1], jnp.where(request == 2 * j + 1, own[1:2], 0.0)
        )
        s["r_send"][n] = part.astype(BF).reshape(2, 16, BLK)
        for h in range(2):

            @pl.when(jnp.logical_not(r_mine(n, h)))
            def _():
                r_copy(n, h).start()

            @pl.when(r_mine(n, h))
            def _():
                s["r_recv"][j] = s["r_send"][n, h]

        return carry

    lax.fori_loop(0, 8, r_start, 0)

    def m_wait(k, carry):
        m_copy(k, lax.rem(j + 16 - k, 16)).wait_recv()
        return carry

    lax.fori_loop(1, 16, m_wait, 0)
    s["m_all"][i] = jnp.sum(s["m_one"][...], axis=1)

    def n_copy(k, land):
        t = lax.rem(i + k, 8)
        return remote(s["m_all"].at[land], s["m_all"].at[land], s["n_s"].at[k], s["n_r"].at[k], (t, j))

    def n_start(k, carry):
        n_copy(k, i).start()
        return carry

    lax.fori_loop(1, 8, n_start, 0)

    def r_wait(t, carry):
        @pl.when(jnp.logical_not((lax.div(y, 2) == c) & (t == j)))
        def _():
            remote(s["r_send"].at[0, 0], s["r_recv"].at[t], s["r_s"].at[0], s["r_r"].at[t], sibling).wait_recv()

        return carry

    lax.fori_loop(0, 16, r_wait, 0)
    block = jnp.zeros((16, BLK), F32)
    for t in range(16):
        block = block + s["r_recv"][t].astype(F32)
    block = block.astype(BF)
    pieces = (s["xa"], s["xb"], s["xc"])
    for p in range(3):
        pieces[p][z, x, y] = block[:, STARTS[p] : STARTS[p] + PIECES[p]]

    def view(p, whole, fixed):
        where = [slice(None) if a in whole else fixed.get(a, at[a]) for a in ("z", "x", "y")]
        return pieces[p].at[tuple(where)]

    def g_copy(step, p, k, landing):
        axis = GATHER[p][step]
        fixed = {axis: turn(axis, 4 - k)} if landing else {}
        ref = view(p, GATHER[p][:step], fixed)
        return remote(
            ref, ref, s["g_s"].at[step, p, k], s["g_r"].at[step, p, k], place(axis, turn(axis, k), c)
        )

    def h_copy(p, kk, k, landing):
        axis = GATHER[p][2]
        fixed = {axis: turn(axis, 4 - k)} if landing else {}
        if axis != "z":
            fixed["z"] = turn("z", kk)
        ref = view(p, [a for a in ("x", "y") if a != axis], fixed)
        return remote(ref, ref, s["h_s"].at[p, kk, k], s["h_r"].at[p, kk, k], place(axis, turn(axis, k), c))

    for step in range(2):
        for p in range(3):
            if step:
                for k in (1, 2, 3):
                    g_copy(step - 1, p, k, True).wait_recv()
            for k in (1, 2, 3):
                g_copy(step, p, k, False).start()
    for p in (2, 0, 1):
        for k in (1, 2, 3):
            g_copy(1, p, k, True).wait_recv()
        for kk in range(4 if p < 2 else 1):
            for k in (1, 2, 3):
                h_copy(p, kk, k, False).start()

    def n_wait(k, carry):
        n_copy(k, lax.rem(i + 8 - k, 8)).wait_recv()
        return carry

    lax.fori_loop(1, 8, n_wait, 0)
    notes = s["m_all"][...].reshape(128, 128)
    notes_high = notes.astype(BF)
    notes_low = (notes - notes_high.astype(F32)).astype(BF)
    picked = dot_nt(ones_where(iota((8, 128), 1) == 32 + iota((8, 128), 0)), notes_high).astype(BF)
    picked = dot(picked, ones_where(lax.div(iota((128, 256), 1), 2) == iota((128, 256), 0)))
    home = iota((1, 256), 1)
    home_key = jnp.where(
        picked[0:1] == lax.rem(home, 2).astype(F32),
        256.0 + picked[1:2] * 16.0 + lax.rem(lax.div(home, 2), 16).astype(F32),
        home.astype(F32),
    )

    def arrange(device, slot):
        size = device.shape[0]
        lanes = iota((size, 128), 1)
        found = ones_where(lanes == device)
        found = dot(found, notes_high) + dot(found, notes_low)
        weigh = jnp.sum(jnp.where(lanes == slot * 16 + j, found, 0.0), axis=1, keepdims=True)
        leaving = jnp.sum(jnp.where(lanes == 32, found, 0.0), axis=1, keepdims=True)
        key = jnp.where(
            leaving == slot.astype(F32), 256.0 + device.astype(F32), (2 * device + slot).astype(F32)
        )
        return ones_where(key == home_key), weigh

    t = iota((256, 1), 0)
    for p in range(3):
        coords = {
            REDUCE[p][0]: lax.div(t, 64),
            REDUCE[p][1]: lax.rem(lax.div(t, 16), 4),
            REDUCE[p][2]: lax.rem(lax.div(t, 4), 4),
        }
        device = (coords["x"] * 2 + lax.rem(lax.div(t, 2), 2)) * 16 + coords["z"] * 4 + coords["y"]
        matrix, weigh = arrange(device, lax.rem(t, 2))
        s["perm"][p] = matrix
        s["weight"][p] = jnp.broadcast_to(weigh, (256, 128))
    t = iota((16, 1), 0)
    chosen, _ = arrange((x * 2 + lax.rem(lax.div(t, 2), 2)) * 16 + j, lax.rem(t, 2))

    for n in range(13, 15):
        loads[n].wait()
    for n in range(2):
        swaps[n].wait_recv()
    s["pre"][...] = jnp.zeros((4, 256, 256), F32)
    s["squares"][...] = jnp.zeros((256, 128), F32)

    def project(kk, carry):
        zz = turn("z", kk)
        for p in range(2):
            for k in (1, 2, 3):
                h_copy(p, kk, k, True).wait_recv()

        @pl.when(kk > 0)
        def _():
            h_copy(2, 0, 4 - kk, True).wait_recv()

        squares = s["squares"][...]
        for p in range(3):
            rows = pieces[p][zz].reshape(256, PIECES[p]).astype(F32)
            for n in range(PIECES[p] // 128):
                tile = rows[:, 128 * n : 128 * n + 128]
                squares = squares + tile * tile
            width = pl.multiple_of(c * HALF + zz * BLK + STARTS[p], 128)
            s["xg"][:, STARTS[p] : STARTS[p] + PIECES[p]] = (
                rows * gain[:, pl.ds(width, PIECES[p])]
            ).astype(BF)
        s["squares"][...] = squares
        depth = pl.multiple_of(zz * BLK, 128)
        for m in range(4):
            s["pre"][m] = s["pre"][m] + dot(s["xg"][...], s["wv"][m, pl.ds(depth, BLK), :])
        return carry

    lax.fori_loop(0, 4, project, 0)

    halves = [
        remote(s["pre_send"].at[m], s["pre_recv"].at[(m + 2) % 4], s["swap_s"].at[3 + m], s["swap_r"].at[3 + (m + 2) % 4], sibling)
        for m in range(4)
    ]
    sums = remote(s["squares"], s["squares_in"], s["swap_s"].at[7], s["swap_r"].at[7], sibling)
    sums.start()
    for m in (2, 3, 0, 1):
        s["pre_send"][m] = s["pre"][m].astype(BF)
        halves[m].start()
    sums.wait_recv()
    square = jnp.sum(s["squares"][...] + s["squares_in"][...], axis=1, keepdims=True)
    norm = lax.rsqrt(square / D + 1e-06)
    for b in range(2):
        halves[(2 * b + 2) % 4].wait_recv()
        halves[(2 * b + 3) % 4].wait_recv()
        gate = (s["pre"][2 * b] + s["pre_recv"][2 * b].astype(F32)) * norm
        up = (s["pre"][2 * b + 1] + s["pre_recv"][2 * b + 1].astype(F32)) * norm
        s["inner"][b] = (gate / (1.0 + jnp.exp(-gate)) * up).astype(BF)
    for p in range(3):
        weigh = s["weight"][p][:, 0:1]
        for b in range(2):
            s["sorted_in"][p, b] = (dot(s["perm"][p], s["inner"][b]) * weigh).astype(BF)

    def c_copy(n, p, k, landing):
        axis = REDUCE[p][0]
        return remote(
            s["c_send"].at[n, turn(axis, k)],
            s["c_recv"].at[n, k],
            s["c_s"].at[n, k],
            s["c_r"].at[n, k],
            place(axis, turn(axis, k), c),
        )

    def b_copy(n, p, k, landing):
        axis = REDUCE[p][1]
        return remote(
            s["b_send"].at[n, turn(axis, k)],
            s["b_recv"].at[n, k],
            s["b_s"].at[n, k],
            s["b_r"].at[n, k],
            place(axis, turn(axis, k), c),
        )

    loads[15].wait()
    swaps[2].wait_recv()
    for p, q in CHUNKS:
        n = BASE[p] + q
        cols = slice(256 * n, 256 * n + 256)
        part = dot(s["sorted_in"][p, 0], s["wd"][0, :, cols]) + dot(s["sorted_in"][p, 1], s["wd"][1, :, cols])
        s["c_send"][n] = part.astype(BF).reshape(4, 64, 256)
        for k in (1, 2, 3):
            c_copy(n, p, k, False).start()

    for p in range(3):
        for zz in range(4):
            begin = zz * BLK + STARTS[p]
            s["resid"][:, begin : begin + PIECES[p]] = dot(chosen, pieces[p][zz].reshape(256, PIECES[p]))

    for p, q in CHUNKS:
        n = BASE[p] + q
        axis = REDUCE[p][0]
        for k in (1, 2, 3):
            c_copy(n, p, k, True).wait_recv()
        part = s["c_send"][n, at[axis]].astype(F32)
        for k in (1, 2, 3):
            part = part + s["c_recv"][n, k].astype(F32)
        s["b_send"][n] = part.astype(BF).reshape(4, 16, 256)
        for k in (1, 2, 3):
            b_copy(n, p, k, False).start()

    def f_copy(p, m, landing):
        axis = REDUCE[p][2]
        mine = at[axis] * 2 + c
        t = lax.rem(mine + m, 8)
        wide = pl.ds(0, COUNT[p] * 256)
        land = lax.rem(mine + 8 - m, 8) if landing else mine
        return remote(
            s["f_send"].at[p, t, :, wide],
            s["f_recv"].at[p, land, :, wide],
            s["f_s"].at[p, m],
            s["f_r"].at[p, m],
            place(axis, lax.div(t, 2), lax.rem(t, 2)),
        )

    last = lax.div(iota((16, 1), 0), 4)
    for p, q in CHUNKS:
        n = BASE[p] + q
        for k in (1, 2, 3):
            b_copy(n, p, k, True).wait_recv()
        part = s["b_send"][n, at[REDUCE[p][1]]].astype(F32)
        for k in (1, 2, 3):
            part = part + s["b_recv"][n, k].astype(F32)
        part = part + jnp.where(last == at[REDUCE[p][2]], s["resid"][:, 256 * n : 256 * n + 256], 0.0)
        for t in range(8):
            s["f_send"][p, t, :, 256 * q : 256 * q + 256] = part[2 * t : 2 * t + 2]
        if q == COUNT[p] - 1:
            for m in range(1, 8):
                f_copy(p, m, False).start()
            mine = at[REDUCE[p][2]] * 2 + c
            s["f_recv"][p, mine] = s["f_send"][p, mine]
    for p in (2, 0, 1):
        for m in range(1, 8):
            f_copy(p, m, True).wait_recv()
        for core in range(2):
            part = s["f_recv"][p, core]
            for t in range(1, 4):
                part = part + s["f_recv"][p, 2 * t + core]
            wide = COUNT[p] * 256
            begin = core * HALF + BASE[p] * 256
            out[:, begin : begin + wide] = part[:, :wide].astype(BF)

    def a_done(k, carry):
        a_copy(k, j).wait_send()
        m_copy(k, j).wait_send()
        return carry

    lax.fori_loop(1, 16, a_done, 0)

    def n_done(k, carry):
        n_copy(k, i).wait_send()
        return carry

    lax.fori_loop(1, 8, n_done, 0)

    def r_done(n, carry):
        for h in range(2):

            @pl.when(jnp.logical_not(r_mine(n, h)))
            def _():
                r_copy(n, h).wait_send()

        return carry

    lax.fori_loop(0, 8, r_done, 0)
    for copy in swaps + halves + [sums]:
        copy.wait_send()
    for p in range(3):
        for k in (1, 2, 3):
            for step in range(2):
                g_copy(step, p, k, False).wait_send()
            for kk in range(4 if p < 2 else 1):
                h_copy(p, kk, k, False).wait_send()
        for m in range(1, 8):
            f_copy(p, m, False).wait_send()
    for p, q in CHUNKS:
        for k in (1, 2, 3):
            c_copy(BASE[p] + q, p, k, False).wait_send()
            b_copy(BASE[p] + q, p, k, False).wait_send()


def on_device(
    hidden,
    q_latent,
    q_rope,
    latent_pages,
    rope_pages,
    block_table,
    cache_len,
    move_req,
    move_to,
    routing,
    gate_weight,
    norm_gain,
    w_uv,
    w_out,
    w_gate,
    w_up,
    w_down,
):
    vmem = pl.BlockSpec(memory_space=pltpu.VMEM)
    smem = pl.BlockSpec(memory_space=pltpu.SMEM)
    hbm = pl.BlockSpec(memory_space=pl.ANY)
    return pl.pallas_call(
        layer,
        out_shape=jax.ShapeDtypeStruct((2, D), BF),
        in_specs=[vmem] * 2 + [smem] * 6 + [hbm] * 9,
        out_specs=vmem,
        scratch_shapes=list(SCRATCH.values()),
        compiler_params=pltpu.CompilerParams(
            collective_id=0, has_side_effects=True, vmem_limit_bytes=56 * 1024 * 1024
        ),
        cost_estimate=pl.CostEstimate(flops=4_000_000_000, bytes_accessed=22_000_000, transcendentals=400_000),
    )(
        hidden,
        norm_gain.reshape(1, D),
        block_table,
        cache_len,
        move_req,
        move_to,
        routing,
        gate_weight,
        q_latent,
        q_rope,
        latent_pages,
        rope_pages,
        w_uv,
        w_out,
        w_gate,
        w_up,
        w_down,
    )


def solution(mesh):
    placed = (
        P(("dp", "ep"), None),
        P(("dp", "ep"), None, None),
        P(("dp", "ep"), None, None),
        P(("dp", "ep"), None, None),
        P(("dp", "ep"), None, None),
        P(("dp", "ep"), None),
        P(("dp", "ep")),
        P(("dp", "ep")),
        P(("dp", "ep")),
        P(("dp", "ep"), None),
        P(("dp", "ep"), None),
        P(),
        P("ep", None, None),
        P("ep", None),
        P("ep", None, "dp"),
        P("ep", None, "dp"),
        P("ep", "dp", None),
    )
    return jax.shard_map(
        on_device, mesh=mesh, in_specs=placed, out_specs=P(("dp", "ep"), None), check_vma=False
    )
```

```python
import types

import jax
import jax.numpy as jnp
from jax import lax
from jax.experimental import pallas as pl
from jax.experimental.pallas import tpu as pltpu
from jax.sharding import PartitionSpec as P

MESH = pl.DeviceIdType.MESH
BF = jnp.bfloat16
F32 = jnp.float32

D = 7168
HALF = D // 2
BLK = 896
PIECES = (384, 256, 256)
STARTS = (0, 384, 640)
GATHER = (("z", "y", "x"), ("z", "x", "y"), ("x", "y", "z"))
REDUCE = (("x", "y", "z"), ("y", "z", "x"), ("z", "x", "y"))
BASE = (0, 5, 10)
COUNT = (5, 5, 4)
DIRECT = 1
CHUNKS = [(p, q) for q in range(5) for p in range(3) if q < COUNT[p]]

SCRATCH = dict(
    qv=pltpu.VMEM((2, 64, 512), BF),
    qrv=pltpu.VMEM((2, 64, 64), BF),
    pgv=pltpu.VMEM((24, 64, 512), BF),
    rpv=pltpu.VMEM((24, 32, 128), BF),
    uvv=pltpu.VMEM((4, 512, 128), BF),
    wov=pltpu.VMEM((8, 512, BLK), BF),
    wv=pltpu.VMEM((4, HALF, 256), BF),
    wd=pltpu.VMEM((2, 256, HALF), BF),
    scores=pltpu.VMEM((6, 128, 256), F32),
    a_send=pltpu.VMEM((16, 16, 256), BF),
    a_recv=pltpu.VMEM((16, 16, 256), BF),
    ra_send=pltpu.VMEM((16, 16, PIECES[0]), BF),
    rb_send=pltpu.VMEM((16, 16, PIECES[1]), BF),
    rc_send=pltpu.VMEM((16, 16, PIECES[2]), BF),
    ra_recv=pltpu.VMEM((16, 16, PIECES[0]), BF),
    rb_recv=pltpu.VMEM((16, 16, PIECES[1]), BF),
    rc_recv=pltpu.VMEM((16, 16, PIECES[2]), BF),
    m_one=pltpu.VMEM((16, 8, 128), F32),
    m_all=pltpu.VMEM((8, 16, 128), F32),
    xa=pltpu.VMEM((4, 4, 4, 16, PIECES[0]), BF),
    xb=pltpu.VMEM((4, 4, 4, 16, PIECES[1]), BF),
    xc=pltpu.VMEM((4, 4, 4, 16, PIECES[2]), BF),
    xg=pltpu.VMEM((256, BLK), BF),
    pre=pltpu.VMEM((4, 256, 256), F32),
    squares=pltpu.VMEM((256, 128), F32),
    squares_in=pltpu.VMEM((256, 128), F32),
    pre_send=pltpu.VMEM((4, 256, 256), BF),
    pre_recv=pltpu.VMEM((4, 256, 256), BF),
    inner=pltpu.VMEM((2, 256, 256), BF),
    sorted_in=pltpu.VMEM((3, 2, 256, 256), BF),
    perm=pltpu.VMEM((3, 256, 256), BF),
    weight=pltpu.VMEM((3, 256, 128), F32),
    resid=pltpu.VMEM((16, HALF), F32),
    c_send=pltpu.VMEM((14, 4, 64, 256), BF),
    c_recv=pltpu.VMEM((14, 3, 64, 256), BF),
    b_send=pltpu.VMEM((14, 4, 16, 256), BF),
    b_recv=pltpu.VMEM((14, 3, 16, 256), BF),
    f_send=pltpu.VMEM((3, 8, 2, 1280), F32),
    f_recv=pltpu.VMEM((3, 8, 2, 1280), F32),
    d_send=pltpu.VMEM((3, 32, 2, 256 * DIRECT), F32),
    d_recv=pltpu.VMEM((3, 32, 2, 256 * DIRECT), F32),
    load_sem=pltpu.SemaphoreType.DMA((8,)),
    swap_s=pltpu.SemaphoreType.DMA((1,)),
    swap_r=pltpu.SemaphoreType.DMA((2,)),
    half_s=pltpu.SemaphoreType.DMA((2,)),
    half_r=pltpu.SemaphoreType.DMA((3,)),
    spread_s=pltpu.SemaphoreType.DMA((3,)),
    spread_r=pltpu.SemaphoreType.DMA((3,)),
    r_s=pltpu.SemaphoreType.DMA((3,)),
    r_r=pltpu.SemaphoreType.DMA((3,)),
    g_s=pltpu.SemaphoreType.DMA((3,)),
    g_r=pltpu.SemaphoreType.DMA((3, 4)),
    h_s=pltpu.SemaphoreType.DMA((3,)),
    h_r=pltpu.SemaphoreType.DMA((3, 4)),
    c_s=pltpu.SemaphoreType.DMA((1,)),
    c_r=pltpu.SemaphoreType.DMA((14,)),
    b_s=pltpu.SemaphoreType.DMA((1,)),
    b_r=pltpu.SemaphoreType.DMA((14,)),
    f_s=pltpu.SemaphoreType.DMA((3,)),
    f_r=pltpu.SemaphoreType.DMA((3,)),
    d_s=pltpu.SemaphoreType.DMA((3,)),
    d_r=pltpu.SemaphoreType.DMA((3,)),
)


def iota(shape, dim):
    return lax.broadcasted_iota(jnp.int32, shape, dim)


def ones_where(mask):
    return jnp.where(mask, 1.0, 0.0).astype(BF)


def dot(a, b):
    return jnp.dot(a, b, preferred_element_type=F32)


def dot_nt(a, b):
    return lax.dot_general(a, b, (((1,), (1,)), ((), ())), preferred_element_type=F32)


def layer(
    hidden,
    gain,
    table,
    lens,
    move_req,
    move_to,
    routing,
    gates,
    q_latent,
    q_rope,
    pages,
    ropes,
    w_uv,
    w_out,
    w_gate,
    w_up,
    w_down,
    out,
    *scratch,
):
    s = types.SimpleNamespace(**dict(zip(SCRATCH, scratch)))
    i = lax.axis_index("dp")
    j = lax.axis_index("ep")
    x, c = lax.div(i, 2), lax.rem(i, 2)
    z, y = lax.div(j, 4), lax.rem(j, 4)
    other = 1 - c
    at = {"x": x, "y": y, "z": z}

    def place(axis, value, core):
        if axis == "x":
            return (value * 2 + core, j)
        if axis == "y":
            return (x * 2 + core, z * 4 + value)
        return (x * 2 + core, value * 4 + y)

    def turn(axis, k):
        return lax.rem(at[axis] + k, 4)

    def remote(src, dst, send, recv, device):
        return pltpu.make_async_remote_copy(
            src_ref=src, dst_ref=dst, send_sem=send, recv_sem=recv, device_id=device, device_id_type=MESH
        )

    sibling = (x * 2 + other, j)

    def loaded(ref, n):
        pltpu.make_async_copy(ref, ref, s.load_sem.at[n]).wait()

    def arrived(ref, sem):
        remote(ref, ref, sem, sem, sibling).wait_recv()

    def sent(ref, sem):
        remote(ref, ref, sem, sem, sibling).wait_send()

    half = pl.multiple_of(c * HALF, 128)
    others = pl.multiple_of(other * HALF, 128)

    def load(src, dst, n):
        pltpu.make_async_copy(src, dst, s.load_sem.at[n]).start()

    load(q_latent, s.qv, 0)
    load(q_rope, s.qrv, 1)
    load(ropes, s.rpv, 2)
    load(pages, s.pgv, 3)

    barrier = pltpu.get_barrier_semaphore()

    def greet(m, carry):
        t = lax.rem(c * 16 + j + m, 32)
        pl.semaphore_signal(
            barrier, inc=1, device_id=(x * 2 + lax.div(t, 16), lax.rem(t, 16)), device_id_type=MESH
        )
        return carry

    lax.fori_loop(1, 32, greet, 0)
    for k in (1, 2, 3):
        for core in (0, 1):
            pl.semaphore_signal(barrier, inc=1, device_id=place("x", turn("x", k), core), device_id_type=MESH)
        for m in (1, 2, 3):
            for core in (0, 1):
                chip = turn("x", k) * 2 + core
                pl.semaphore_signal(barrier, inc=1, device_id=(chip, turn("z", m) * 4 + y), device_id_type=MESH)
                pl.semaphore_signal(barrier, inc=1, device_id=(chip, z * 4 + turn("y", m)), device_id_type=MESH)

    row = iota((128, 128), 0)
    col = iota((128, 128), 1)
    wanted = lax.rem(lax.div(row, 4), 2) * 64 + lax.div(row, 8) * 4 + lax.rem(row, 4)
    order = ones_where(col == wanted)
    twice = ones_where(iota((64, 128), 0) == lax.rem(iota((64, 128), 1), 64))
    first_row = lax.rem(lax.div(iota((128, 1), 0), 4), 2) == 0
    spread = ones_where(lax.div(iota((256, 128), 0), 2) == iota((256, 128), 1))
    parity = lax.div(iota((256, 128), 1), 64) == lax.rem(iota((256, 128), 0), 2)
    place_of = iota((1, 1536), 1)
    bias = []
    for r in range(2):
        live = jnp.zeros((1, 1536), jnp.int32)
        for q in range(12):
            start = table[r, q] * 64
            count = jnp.clip(lens[r] - q * 64, 0, 64)
            live = jnp.where((place_of >= start) & (place_of < start + count), 1, live)
        bias.append(jnp.where(live > 0, 0.0, -1e30))
    scale = 192.0 ** (-0.5)
    loaded(s.qv, 0)
    loaded(s.qrv, 1)
    query = dot(order, s.qv[...].reshape(128, 512)).astype(BF)
    rotary = dot(dot(order, s.qrv[...].reshape(128, 64)).astype(BF), twice).astype(BF)
    loaded(s.rpv, 2)
    loaded(s.pgv, 3)
    load(w_uv, s.uvv, 4)
    for n in range(8):
        load(w_out.at[:, pl.ds(n * BLK, BLK)], s.wov.at[n], 5)
    load(w_gate.at[0, pl.ds(half, HALF), :], s.wv.at[0], 6)
    load(w_up.at[0, pl.ds(half, HALF), :], s.wv.at[1], 6)
    load(w_down.at[0, :, pl.ds(half, HALF)], s.wd.at[0], 7)
    largest = jnp.full((128, 1), -1e30, F32)
    for n in range(6):
        keys = s.pgv[4 * n : 4 * n + 4].reshape(256, 512)
        turned = dot(spread, s.rpv[4 * n : 4 * n + 4].reshape(128, 128))
        turned = jnp.where(parity, turned, 0.0).astype(BF)
        score = (dot_nt(query, keys) + dot_nt(rotary, turned)) * scale
        cut = slice(256 * n, 256 * n + 256)
        score = score + jnp.where(first_row, bias[0][:, cut], bias[1][:, cut])
        s.scores[n] = score
        largest = jnp.maximum(largest, jnp.max(score, axis=1, keepdims=True))
    total = jnp.zeros((128, 1), F32)
    mixed = jnp.zeros((128, 512), F32)
    for n in range(6):
        prob = jnp.exp(s.scores[n] - largest)
        total = total + jnp.sum(prob, axis=1, keepdims=True)
        mixed = mixed + dot(prob.astype(BF), s.pgv[4 * n : 4 * n + 4].reshape(256, 512))
    mixed = mixed / total
    lower = mixed[:, :256].reshape(16, 8, 256)
    upper = mixed[:, 256:].reshape(16, 8, 256)
    s.a_send[...] = jnp.concatenate([lower, upper], axis=1).astype(BF)
    s.a_recv[j] = s.a_send[j]

    pl.semaphore_wait(barrier, 73)

    def a_copy(k, land):
        t = lax.rem(j + k, 16)
        return remote(s.a_send.at[t], s.a_recv.at[land], s.spread_s.at[0], s.spread_r.at[0], (i, t))

    def a_start(k, carry):
        a_copy(k, j).start()
        return carry

    lax.fori_loop(1, 16, a_start, 0)

    lane = iota((8, 128), 1)
    note = jnp.zeros((8, 128), F32)
    for r in range(2):
        for k in range(8):
            note = jnp.where(lane == routing[r, k] + 16 * r, gates[r, k], note)
    note = jnp.where(lane == 32, move_req[0].astype(F32), note)
    note = jnp.where(lane == 33, move_to[0].astype(F32), note)
    s.m_one[j] = jnp.where(iota((8, 128), 0) == 0, note, 0.0)

    def m_copy(k, land):
        t = lax.rem(j + k, 16)
        return remote(s.m_one.at[land], s.m_one.at[land], s.spread_s.at[1], s.spread_r.at[1], (i, t))

    def m_start(k, carry):
        m_copy(k, j).start()
        return carry

    lax.fori_loop(1, 16, m_start, 0)

    swaps = [
        (w_gate.at[0, pl.ds(others, HALF), :], s.wv.at[2]),
        (w_up.at[0, pl.ds(others, HALF), :], s.wv.at[3]),
        (w_down.at[0, :, pl.ds(others, HALF)], s.wd.at[1]),
    ]
    for n, (src, dst) in enumerate(swaps):
        remote(src, dst, s.swap_s.at[0], s.swap_r.at[n // 2], sibling).start()

    target = iota((256, 256), 0)
    inside = lax.rem(target, 128)
    wanted = (
        lax.div(lax.rem(inside, 32), 2) * 16
        + lax.div(target, 128) * 8
        + lax.rem(inside, 2) * 4
        + lax.div(inside, 32)
    )
    by_head = ones_where(iota((256, 256), 1) == wanted)
    loaded(s.uvv, 4)
    arrived(s.a_recv.at[0:15], s.spread_r.at[0])
    grouped = dot(by_head, s.a_recv[...].reshape(256, 256)).astype(BF)
    values = []
    for h in range(4):
        low = grouped[32 * h : 32 * h + 32]
        high = grouped[128 + 32 * h : 160 + 32 * h]
        values.append((dot(low, s.uvv[h, :256]) + dot(high, s.uvv[h, 256:])).astype(BF))
    values = jnp.concatenate(values, axis=1)
    loaded(s.wov, 5)
    request = iota((32, 1), 0)

    r_send = (s.ra_send, s.rb_send, s.rc_send)
    r_recv = (s.ra_recv, s.rb_recv, s.rc_recv)
    keeps = lax.div(y, 2) == c

    def r_start(p):
        wide = PIECES[p]

        def step(t, carry):
            core, zz = lax.rem(lax.div(t, 4) + y, 2), lax.rem(z + t, 4)
            n = core * 4 + zz
            part = dot(values, s.wov[n, :, STARTS[p] : STARTS[p] + wide])
            own = hidden[:, pl.ds(pl.multiple_of(n * BLK + STARTS[p], 128), wide)].astype(F32)
            part = part + jnp.where(
                request == 2 * j, own[0:1], jnp.where(request == 2 * j + 1, own[1:2], 0.0)
            )
            part = part.astype(BF)
            for h in range(2):
                r_send[p][2 * n + h] = part[16 * h : 16 * h + 16]
            for turned in range(2):
                h = lax.rem(lax.div(y, 2) + turned, 2)
                mine = (core == c) & (zz == z) & (2 * c + h == y)

                @pl.when(jnp.logical_not(mine))
                def _():
                    device = (x * 2 + core, zz * 4 + 2 * c + h)
                    remote(r_send[p].at[2 * n + h], r_recv[p].at[j], s.r_s.at[p], s.r_r.at[p], device).start()

                @pl.when(mine)
                def _():
                    r_recv[p][j] = r_send[p][2 * n + h]

            return carry

        lax.fori_loop(0, 8, step, 0)

    for p in range(3):
        r_start(p)

    arrived(s.m_one.at[0:15], s.spread_r.at[1])
    s.m_all[i] = jnp.sum(s.m_one[...], axis=1)

    def n_copy(k, land):
        t = lax.rem(i + k, 8)
        return remote(s.m_all.at[land], s.m_all.at[land], s.spread_s.at[2], s.spread_r.at[2], (t, j))

    def n_start(k, carry):
        n_copy(k, i).start()
        return carry

    lax.fori_loop(1, 8, n_start, 0)

    pieces = (s.xa, s.xb, s.xc)

    def r_sum(p):
        @pl.when(keeps)
        def _():
            arrived(r_recv[p].at[0:15], s.r_r.at[p])

        @pl.when(jnp.logical_not(keeps))
        def _():
            arrived(r_recv[p], s.r_r.at[p])

        block = r_recv[p][0].astype(F32)
        for t in range(1, 16):
            block = block + r_recv[p][t].astype(F32)
        pieces[p][z, x, y] = block.astype(BF)

    def view(p, where):
        return pieces[p].at[tuple(where.get(a, slice(None)) for a in ("z", "x", "y"))]

    def g_start(p):
        first, second, _ = GATHER[p]
        ref = pieces[p].at[z, x, y]
        for m in (2, 1, 3, 0):
            for k in (2, 1, 3, 0):
                if m or k:
                    to = dict(at)
                    to[first], to[second] = turn(first, m), turn(second, k)
                    device = (to["x"] * 2 + c, to["z"] * 4 + to["y"])
                    remote(ref, ref, s.g_s.at[p], s.g_r.at[p, (4 - m) % 4], device).start()

    def h_start(p, m):
        first, _, axis = GATHER[p]
        arrived(r_recv[p].at[0 : 4 if m else 3], s.g_r.at[p, m])
        ref = view(p, {first: turn(first, m), axis: at[axis]})
        for k in (2, 1, 3):
            recv = s.h_r.at[p, 4 - k if axis == "z" else m]
            remote(ref, ref, s.h_s.at[p], recv, place(axis, turn(axis, k), c)).start()

    r_sum(0)
    g_start(0)
    r_sum(1)
    g_start(1)
    h_start(0, 0)
    r_sum(2)
    g_start(2)
    h_start(0, 1)
    h_start(0, 3)
    h_start(1, 0)
    h_start(0, 2)
    h_start(1, 1)
    h_start(1, 3)
    h_start(2, 0)
    h_start(1, 2)
    h_start(2, 1)
    h_start(2, 3)
    h_start(2, 2)

    arrived(s.m_all.at[0:7], s.spread_r.at[2])
    notes = s.m_all[...].reshape(128, 128)
    notes_high = notes.astype(BF)
    notes_low = (notes - notes_high.astype(F32)).astype(BF)
    picked = dot_nt(ones_where(iota((8, 128), 1) == 32 + iota((8, 128), 0)), notes_high).astype(BF)
    picked = dot(picked, ones_where(lax.div(iota((128, 256), 1), 2) == iota((128, 256), 0)))
    home = iota((1, 256), 1)
    home_key = jnp.where(
        picked[0:1] == lax.rem(home, 2).astype(F32),
        256.0 + picked[1:2] * 16.0 + lax.rem(lax.div(home, 2), 16).astype(F32),
        home.astype(F32),
    )

    def arrange(device, slot):
        size = device.shape[0]
        lanes = iota((size, 128), 1)
        found = ones_where(lanes == device)
        found = dot(found, notes_high) + dot(found, notes_low)
        weigh = jnp.sum(jnp.where(lanes == slot * 16 + j, found, 0.0), axis=1, keepdims=True)
        leaving = jnp.sum(jnp.where(lanes == 32, found, 0.0), axis=1, keepdims=True)
        key = jnp.where(
            leaving == slot.astype(F32), 256.0 + device.astype(F32), (2 * device + slot).astype(F32)
        )
        return ones_where(key == home_key), weigh

    t = iota((256, 1), 0)
    for p in range(3):
        coords = {
            REDUCE[p][0]: lax.div(t, 64),
            REDUCE[p][1]: lax.rem(lax.div(t, 16), 4),
            REDUCE[p][2]: lax.rem(lax.div(t, 4), 4),
        }
        device = (coords["x"] * 2 + lax.rem(lax.div(t, 2), 2)) * 16 + coords["z"] * 4 + coords["y"]
        matrix, weigh = arrange(device, lax.rem(t, 2))
        s.perm[p] = matrix
        s.weight[p] = jnp.broadcast_to(weigh, (256, 128))
    t = iota((16, 1), 0)
    chosen, _ = arrange((x * 2 + lax.rem(lax.div(t, 2), 2)) * 16 + j, lax.rem(t, 2))

    loaded(s.wv.at[0:2], 6)
    arrived(s.wv.at[2:4], s.swap_r.at[0])
    s.pre[...] = jnp.zeros((4, 256, 256), F32)
    s.squares[...] = jnp.zeros((256, 128), F32)

    def project(kk, carry):
        zz = turn("z", kk)
        for p in range(2):
            arrived(pieces[p].at[0, 0:3], s.h_r.at[p, kk])

        @pl.when(kk > 0)
        def _():
            arrived(pieces[2].at[0], s.h_r.at[2, kk])

        squares = s.squares[...]
        for p in range(3):
            rows = pieces[p][zz].reshape(256, PIECES[p]).astype(F32)
            for n in range(PIECES[p] // 128):
                tile = rows[:, 128 * n : 128 * n + 128]
                squares = squares + tile * tile
            width = pl.multiple_of(c * HALF + zz * BLK + STARTS[p], 128)
            s.xg[:, STARTS[p] : STARTS[p] + PIECES[p]] = (
                rows * gain[:, pl.ds(width, PIECES[p])]
            ).astype(BF)
        s.squares[...] = squares
        depth = pl.multiple_of(zz * BLK, 128)
        for m in range(4):
            s.pre[m] = s.pre[m] + dot(s.xg[...], s.wv[m, pl.ds(depth, BLK), :])
        return carry

    lax.fori_loop(0, 4, project, 0)

    remote(s.squares, s.squares_in, s.half_s.at[0], s.half_r.at[0], sibling).start()
    for m in (2, 3, 0, 1):
        t = (m + 2) % 4
        s.pre_send[m] = s.pre[m].astype(BF)
        remote(
            s.pre_send.at[m], s.pre_recv.at[t], s.half_s.at[1], s.half_r.at[1 + t // 2], sibling
        ).start()
    arrived(s.squares_in, s.half_r.at[0])
    square = jnp.sum(s.squares[...] + s.squares_in[...], axis=1, keepdims=True)
    norm = lax.rsqrt(square / D + 1e-06)
    for b in range(2):
        arrived(s.pre_recv.at[2 * b : 2 * b + 2], s.half_r.at[1 + b])
        gate = (s.pre[2 * b] + s.pre_recv[2 * b].astype(F32)) * norm
        up = (s.pre[2 * b + 1] + s.pre_recv[2 * b + 1].astype(F32)) * norm
        s.inner[b] = (gate / (1.0 + jnp.exp(-gate)) * up).astype(BF)
    def c_start(n, p):
        axis = REDUCE[p][0]
        for k in (2, 1, 3):
            src, dst = s.c_send.at[n, turn(axis, k)], s.c_recv.at[n, k - 1]
            remote(src, dst, s.c_s.at[0], s.c_r.at[n], place(axis, turn(axis, k), c)).start()

    def b_start(n, p):
        axis = REDUCE[p][1]
        for k in (2, 1, 3):
            src, dst = s.b_send.at[n, turn(axis, k)], s.b_recv.at[n, k - 1]
            remote(src, dst, s.b_s.at[0], s.b_r.at[n], place(axis, turn(axis, k), c)).start()

    loaded(s.wd.at[0], 7)
    arrived(s.wd.at[1], s.swap_r.at[1])
    for p, q in CHUNKS:
        n = BASE[p] + q
        if q == 0:
            weigh = s.weight[p][:, 0:1]
            for b in range(2):
                s.sorted_in[p, b] = (dot(s.perm[p], s.inner[b]) * weigh).astype(BF)
        cols = slice(256 * n, 256 * n + 256)
        part = dot(s.sorted_in[p, 0], s.wd[0, :, cols]) + dot(s.sorted_in[p, 1], s.wd[1, :, cols])
        s.c_send[n] = part.astype(BF).reshape(4, 64, 256)
        c_start(n, p)

    for p in range(3):
        for zz in range(4):
            begin = zz * BLK + STARTS[p]
            s.resid[:, begin : begin + PIECES[p]] = dot(chosen, pieces[p][zz].reshape(256, PIECES[p]))

    quarter = lax.div(iota((64, 1), 0), 4)

    def d_start(p):
        axis, first, second = REDUCE[p]
        mine = (at[first] * 4 + at[second]) * 2 + c

        def step(m, carry):
            t = lax.rem(mine + m, 32)
            to = {axis: at[axis], first: lax.div(t, 8), second: lax.rem(lax.div(t, 2), 4)}
            device = (to["x"] * 2 + lax.rem(t, 2), to["z"] * 4 + to["y"])
            remote(s.d_send.at[p, t], s.d_recv.at[p, mine], s.d_s.at[p], s.d_r.at[p], device).start()
            return carry

        lax.fori_loop(1, 32, step, 0)
        s.d_recv[p, mine] = s.d_send[p, mine]

    for p, q in CHUNKS:
        n = BASE[p] + q
        axis = REDUCE[p][0]
        arrived(s.c_recv.at[n], s.c_r.at[n])
        part = s.c_send[n, at[axis]].astype(F32)
        for k in range(3):
            part = part + s.c_recv[n, k].astype(F32)
        if q < COUNT[p] - DIRECT:
            s.b_send[n] = part.astype(BF).reshape(4, 16, 256)
            b_start(n, p)
            continue
        stays = jnp.concatenate([s.resid[:, 256 * n : 256 * n + 256]] * 4, axis=0)
        part = part + jnp.where(quarter == at[REDUCE[p][1]] * 4 + at[REDUCE[p][2]], stays, 0.0)
        begin = 256 * (q + DIRECT - COUNT[p])
        for t in range(32):
            s.d_send[p, t, :, begin : begin + 256] = part[2 * t : 2 * t + 2]
        if q == COUNT[p] - 1:
            d_start(p)

    def f_start(p):
        mine = at[REDUCE[p][2]] * 2 + c
        wide = pl.ds(0, (COUNT[p] - DIRECT) * 256)
        for m in range(1, 8):
            t = lax.rem(mine + m, 8)
            src, dst = s.f_send.at[p, t, :, wide], s.f_recv.at[p, mine, :, wide]
            device = place(REDUCE[p][2], lax.div(t, 2), lax.rem(t, 2))
            remote(src, dst, s.f_s.at[p], s.f_r.at[p], device).start()
        s.f_recv[p, mine] = s.f_send[p, mine]

    last = lax.div(iota((16, 1), 0), 4)
    for p, q in CHUNKS:
        if q >= COUNT[p] - DIRECT:
            continue
        n = BASE[p] + q
        arrived(s.b_recv.at[n], s.b_r.at[n])
        part = s.b_send[n, at[REDUCE[p][1]]].astype(F32)
        for k in range(3):
            part = part + s.b_recv[n, k].astype(F32)
        part = part + jnp.where(last == at[REDUCE[p][2]], s.resid[:, 256 * n : 256 * n + 256], 0.0)
        for t in range(8):
            s.f_send[p, t, :, 256 * q : 256 * q + 256] = part[2 * t : 2 * t + 2]
        if q == COUNT[p] - DIRECT - 1:
            f_start(p)
    for p in (2, 0, 1):
        wide = (COUNT[p] - DIRECT) * 256
        arrived(s.f_recv.at[p, 0:7, :, pl.ds(0, wide)], s.f_r.at[p])
        for core in range(2):
            part = s.f_recv[p, core]
            for t in range(1, 4):
                part = part + s.f_recv[p, 2 * t + core]
            begin = core * HALF + BASE[p] * 256
            out[:, begin : begin + wide] = part[:, :wide].astype(BF)
    for p in (2, 0, 1):
        arrived(s.d_recv.at[p, 0:31], s.d_r.at[p])
        for core in range(2):
            part = s.d_recv[p, core]
            for t in range(1, 16):
                part = part + s.d_recv[p, 2 * t + core]
            begin = core * HALF + (BASE[p] + COUNT[p] - DIRECT) * 256
            out[:, begin : begin + 256 * DIRECT] = part.astype(BF)

    sent(s.a_send.at[0:15], s.spread_s.at[0])
    sent(s.m_one.at[0:15], s.spread_s.at[1])
    sent(s.m_all.at[0:7], s.spread_s.at[2])

    for p in range(3):

        @pl.when(keeps)
        def _():
            sent(r_send[p].at[0:15], s.r_s.at[p])

        @pl.when(jnp.logical_not(keeps))
        def _():
            sent(r_send[p], s.r_s.at[p])

    sent(s.wv.at[0:3], s.swap_s.at[0])
    sent(s.squares, s.half_s.at[0])
    sent(s.pre_send, s.half_s.at[1])
    for p in range(3):
        sent(r_recv[p].at[0:15], s.g_s.at[p])
        sent(pieces[p].at[0:3], s.h_s.at[p])
        sent(s.f_send.at[p, 0:7, :, pl.ds(0, (COUNT[p] - DIRECT) * 256)], s.f_s.at[p])
        sent(s.d_send.at[p, 0:31], s.d_s.at[p])
    sent(s.c_send.at[:, 0:3], s.c_s.at[0])
    sent(s.b_send.at[0 : 14 - 3 * DIRECT, 0:3], s.b_s.at[0])


def on_device(
    hidden,
    q_latent,
    q_rope,
    latent_pages,
    rope_pages,
    block_table,
    cache_len,
    move_req,
    move_to,
    routing,
    gate_weight,
    norm_gain,
    w_uv,
    w_out,
    w_gate,
    w_up,
    w_down,
):
    vmem = pl.BlockSpec(memory_space=pltpu.VMEM)
    smem = pl.BlockSpec(memory_space=pltpu.SMEM)
    hbm = pl.BlockSpec(memory_space=pl.ANY)
    return pl.pallas_call(
        layer,
        out_shape=jax.ShapeDtypeStruct((2, D), BF),
        in_specs=[vmem] * 2 + [smem] * 6 + [hbm] * 9,
        out_specs=vmem,
        scratch_shapes=list(SCRATCH.values()),
        compiler_params=pltpu.CompilerParams(
            collective_id=0, has_side_effects=True, vmem_limit_bytes=56 * 1024 * 1024
        ),
        cost_estimate=pl.CostEstimate(flops=4_000_000_000, bytes_accessed=22_000_000, transcendentals=400_000),
    )(
        hidden,
        norm_gain.reshape(1, D),
        block_table,
        cache_len,
        move_req,
        move_to,
        routing,
        gate_weight,
        q_latent,
        q_rope,
        latent_pages,
        rope_pages,
        w_uv,
        w_out,
        w_gate,
        w_up,
        w_down,
    )


def solution(mesh):
    placed = (
        P(("dp", "ep"), None),
        P(("dp", "ep"), None, None),
        P(("dp", "ep"), None, None),
        P(("dp", "ep"), None, None),
        P(("dp", "ep"), None, None),
        P(("dp", "ep"), None),
        P(("dp", "ep")),
        P(("dp", "ep")),
        P(("dp", "ep")),
        P(("dp", "ep"), None),
        P(("dp", "ep"), None),
        P(),
        P("ep", None, None),
        P("ep", None),
        P("ep", None, "dp"),
        P("ep", None, "dp"),
        P("ep", "dp", None),
    )
    return jax.shard_map(
        on_device, mesh=mesh, in_specs=placed, out_specs=P(("dp", "ep"), None), check_vma=False
    )
```

```python
import types

import jax
import jax.numpy as jnp
from jax import lax
from jax.experimental import pallas as pl
from jax.experimental.pallas import tpu as pltpu
from jax.sharding import PartitionSpec as P

MESH = pl.DeviceIdType.MESH
BF = jnp.bfloat16
F32 = jnp.float32

D = 7168
HALF = D // 2
BLK = 896
PIECES = (256, 128, 256, 256)
STARTS = (0, 256, 384, 640)
GATHER = (("z", "y", "x"), ("z", "x", "y"), ("z", "x", "y"), ("x", "y", "z"))
REDUCE = (("x", "y", "z"), ("y", "z", "x"), ("z", "x", "y"))
BASE = (0, 5, 10)
COUNT = (5, 5, 4)
DIRECT = 1
CHUNKS = [(p, q) for q in range(5) for p in range(3) if q < COUNT[p]]

SCRATCH = dict(
    qv=pltpu.VMEM((2, 64, 512), BF),
    qrv=pltpu.VMEM((2, 64, 64), BF),
    pgv=pltpu.VMEM((24, 64, 512), BF),
    rpv=pltpu.VMEM((24, 32, 128), BF),
    uvv=pltpu.VMEM((4, 512, 128), BF),
    wov=pltpu.VMEM((8, 512, BLK), BF),
    wv=pltpu.VMEM((4, HALF, 256), BF),
    wd=pltpu.VMEM((2, 256, HALF), BF),
    scores=pltpu.VMEM((6, 128, 256), F32),
    a_send=pltpu.VMEM((16, 16, 256), BF),
    a_recv=pltpu.VMEM((16, 16, 256), BF),
    ra_send=pltpu.VMEM((16, 16, PIECES[0]), BF),
    rb_send=pltpu.VMEM((16, 16, PIECES[1]), BF),
    rc_send=pltpu.VMEM((16, 16, PIECES[2]), BF),
    rd_send=pltpu.VMEM((16, 16, PIECES[3]), BF),
    ra_recv=pltpu.VMEM((16, 16, PIECES[0]), BF),
    rb_recv=pltpu.VMEM((16, 16, PIECES[1]), BF),
    rc_recv=pltpu.VMEM((16, 16, PIECES[2]), BF),
    rd_recv=pltpu.VMEM((16, 16, PIECES[3]), BF),
    m_one=pltpu.VMEM((16, 8, 128), F32),
    m_all=pltpu.VMEM((8, 16, 128), F32),
    xa=pltpu.VMEM((4, 4, 4, 16, PIECES[0]), BF),
    xb=pltpu.VMEM((4, 4, 4, 16, PIECES[1]), BF),
    xc=pltpu.VMEM((4, 4, 4, 16, PIECES[2]), BF),
    xd=pltpu.VMEM((4, 4, 4, 16, PIECES[3]), BF),
    xg=pltpu.VMEM((256, BLK), BF),
    pre=pltpu.VMEM((4, 256, 256), F32),
    squares=pltpu.VMEM((256, 128), F32),
    squares_in=pltpu.VMEM((256, 128), F32),
    pre_send=pltpu.VMEM((4, 256, 256), BF),
    pre_recv=pltpu.VMEM((4, 256, 256), BF),
    inner=pltpu.VMEM((2, 256, 256), BF),
    sorted_in=pltpu.VMEM((3, 2, 256, 256), BF),
    perm=pltpu.VMEM((3, 256, 256), BF),
    weight=pltpu.VMEM((3, 256, 128), F32),
    resid=pltpu.VMEM((16, HALF), F32),
    c_send=pltpu.VMEM((14, 4, 64, 256), BF),
    c_recv=pltpu.VMEM((14, 3, 64, 256), BF),
    b_send=pltpu.VMEM((14, 4, 16, 256), BF),
    b_recv=pltpu.VMEM((14, 3, 16, 256), BF),
    f_send=pltpu.VMEM((3, 8, 2, 1280), F32),
    f_recv=pltpu.VMEM((3, 8, 2, 1280), F32),
    d_send=pltpu.VMEM((3, 32, 2, 256 * DIRECT), F32),
    d_recv=pltpu.VMEM((3, 32, 2, 256 * DIRECT), F32),
    load_sem=pltpu.SemaphoreType.DMA((8,)),
    swap_s=pltpu.SemaphoreType.DMA((1,)),
    swap_r=pltpu.SemaphoreType.DMA((2,)),
    half_s=pltpu.SemaphoreType.DMA((2,)),
    half_r=pltpu.SemaphoreType.DMA((3,)),
    spread_s=pltpu.SemaphoreType.DMA((3,)),
    spread_r=pltpu.SemaphoreType.DMA((3,)),
    r_s=pltpu.SemaphoreType.DMA((4,)),
    r_r=pltpu.SemaphoreType.DMA((4,)),
    g_s=pltpu.SemaphoreType.DMA((4,)),
    g_r=pltpu.SemaphoreType.DMA((4, 4)),
    h_s=pltpu.SemaphoreType.DMA((4,)),
    h_r=pltpu.SemaphoreType.DMA((4, 4)),
    c_s=pltpu.SemaphoreType.DMA((1,)),
    c_r=pltpu.SemaphoreType.DMA((14,)),
    b_s=pltpu.SemaphoreType.DMA((1,)),
    b_r=pltpu.SemaphoreType.DMA((14,)),
    f_s=pltpu.SemaphoreType.DMA((3,)),
    f_r=pltpu.SemaphoreType.DMA((3,)),
    d_s=pltpu.SemaphoreType.DMA((3,)),
    d_r=pltpu.SemaphoreType.DMA((3,)),
)


def iota(shape, dim):
    return lax.broadcasted_iota(jnp.int32, shape, dim)


def ones_where(mask):
    return jnp.where(mask, 1.0, 0.0).astype(BF)


def dot(a, b):
    return jnp.dot(a, b, preferred_element_type=F32)


def dot_nt(a, b):
    return lax.dot_general(a, b, (((1,), (1,)), ((), ())), preferred_element_type=F32)


def layer(
    hidden,
    gain,
    table,
    lens,
    move_req,
    move_to,
    routing,
    gates,
    q_latent,
    q_rope,
    pages,
    ropes,
    w_uv,
    w_out,
    w_gate,
    w_up,
    w_down,
    out,
    *scratch,
):
    s = types.SimpleNamespace(**dict(zip(SCRATCH, scratch)))
    i = lax.axis_index("dp")
    j = lax.axis_index("ep")
    x, c = lax.div(i, 2), lax.rem(i, 2)
    z, y = lax.div(j, 4), lax.rem(j, 4)
    other = 1 - c
    at = {"x": x, "y": y, "z": z}

    def place(axis, value, core):
        if axis == "x":
            return (value * 2 + core, j)
        if axis == "y":
            return (x * 2 + core, z * 4 + value)
        return (x * 2 + core, value * 4 + y)

    def turn(axis, k):
        return lax.rem(at[axis] + k, 4)

    def remote(src, dst, send, recv, device):
        return pltpu.make_async_remote_copy(
            src_ref=src, dst_ref=dst, send_sem=send, recv_sem=recv, device_id=device, device_id_type=MESH
        )

    sibling = (x * 2 + other, j)

    def loaded(ref, n):
        pltpu.make_async_copy(ref, ref, s.load_sem.at[n]).wait()

    def arrived(ref, sem):
        remote(ref, ref, sem, sem, sibling).wait_recv()

    def sent(ref, sem):
        remote(ref, ref, sem, sem, sibling).wait_send()

    half = pl.multiple_of(c * HALF, 128)
    others = pl.multiple_of(other * HALF, 128)

    def load(src, dst, n):
        pltpu.make_async_copy(src, dst, s.load_sem.at[n]).start()

    load(q_latent, s.qv, 0)
    load(q_rope, s.qrv, 1)
    load(ropes, s.rpv, 2)
    load(pages, s.pgv, 3)

    barrier = pltpu.get_barrier_semaphore()

    def greet(m, carry):
        t = lax.rem(c * 16 + j + m, 32)
        pl.semaphore_signal(
            barrier, inc=1, device_id=(x * 2 + lax.div(t, 16), lax.rem(t, 16)), device_id_type=MESH
        )
        return carry

    lax.fori_loop(1, 32, greet, 0)
    for k in (1, 2, 3):
        for core in (0, 1):
            pl.semaphore_signal(barrier, inc=1, device_id=place("x", turn("x", k), core), device_id_type=MESH)
        for m in (1, 2, 3):
            for core in (0, 1):
                chip = turn("x", k) * 2 + core
                pl.semaphore_signal(barrier, inc=1, device_id=(chip, turn("z", m) * 4 + y), device_id_type=MESH)
                pl.semaphore_signal(barrier, inc=1, device_id=(chip, z * 4 + turn("y", m)), device_id_type=MESH)

    row = iota((128, 128), 0)
    col = iota((128, 128), 1)
    wanted = lax.rem(lax.div(row, 4), 2) * 64 + lax.div(row, 8) * 4 + lax.rem(row, 4)
    order = ones_where(col == wanted)
    twice = ones_where(iota((64, 128), 0) == lax.rem(iota((64, 128), 1), 64))
    first_row = lax.rem(lax.div(iota((128, 1), 0), 4), 2) == 0
    spread = ones_where(lax.div(iota((256, 128), 0), 2) == iota((256, 128), 1))
    parity = lax.div(iota((256, 128), 1), 64) == lax.rem(iota((256, 128), 0), 2)
    place_of = iota((1, 1536), 1)
    bias = []
    for r in range(2):
        live = jnp.zeros((1, 1536), jnp.int32)
        for q in range(12):
            start = table[r, q] * 64
            count = jnp.clip(lens[r] - q * 64, 0, 64)
            live = jnp.where((place_of >= start) & (place_of < start + count), 1, live)
        bias.append(jnp.where(live > 0, 0.0, -1e30))
    scale = 192.0 ** (-0.5)
    loaded(s.qv, 0)
    loaded(s.qrv, 1)
    query = dot(order, s.qv[...].reshape(128, 512)).astype(BF)
    rotary = dot(dot(order, s.qrv[...].reshape(128, 64)).astype(BF), twice).astype(BF)
    loaded(s.rpv, 2)
    loaded(s.pgv, 3)
    load(w_uv, s.uvv, 4)
    for n in range(8):
        load(w_out.at[:, pl.ds(n * BLK, BLK)], s.wov.at[n], 5)
    load(w_gate.at[0, pl.ds(half, HALF), :], s.wv.at[0], 6)
    load(w_up.at[0, pl.ds(half, HALF), :], s.wv.at[1], 6)
    load(w_down.at[0, :, pl.ds(half, HALF)], s.wd.at[0], 7)
    largest = jnp.full((128, 1), -1e30, F32)
    for n in range(6):
        keys = s.pgv[4 * n : 4 * n + 4].reshape(256, 512)
        turned = dot(spread, s.rpv[4 * n : 4 * n + 4].reshape(128, 128))
        turned = jnp.where(parity, turned, 0.0).astype(BF)
        score = (dot_nt(query, keys) + dot_nt(rotary, turned)) * scale
        cut = slice(256 * n, 256 * n + 256)
        score = score + jnp.where(first_row, bias[0][:, cut], bias[1][:, cut])
        s.scores[n] = score
        largest = jnp.maximum(largest, jnp.max(score, axis=1, keepdims=True))
    total = jnp.zeros((128, 1), F32)
    mixed = jnp.zeros((128, 512), F32)
    for n in range(6):
        prob = jnp.exp(s.scores[n] - largest)
        total = total + jnp.sum(prob, axis=1, keepdims=True)
        mixed = mixed + dot(prob.astype(BF), s.pgv[4 * n : 4 * n + 4].reshape(256, 512))
    mixed = mixed / total
    lower = mixed[:, :256].reshape(16, 8, 256)
    upper = mixed[:, 256:].reshape(16, 8, 256)
    s.a_send[...] = jnp.concatenate([lower, upper], axis=1).astype(BF)
    s.a_recv[j] = s.a_send[j]

    pl.semaphore_wait(barrier, 73)

    def a_copy(k, land):
        t = lax.rem(j + k, 16)
        return remote(s.a_send.at[t], s.a_recv.at[land], s.spread_s.at[0], s.spread_r.at[0], (i, t))

    def a_start(k, carry):
        a_copy(k, j).start()
        return carry

    lax.fori_loop(1, 16, a_start, 0)

    lane = iota((8, 128), 1)
    note = jnp.zeros((8, 128), F32)
    for r in range(2):
        for k in range(8):
            note = jnp.where(lane == routing[r, k] + 16 * r, gates[r, k], note)
    note = jnp.where(lane == 32, move_req[0].astype(F32), note)
    note = jnp.where(lane == 33, move_to[0].astype(F32), note)
    s.m_one[j] = jnp.where(iota((8, 128), 0) == 0, note, 0.0)

    def m_copy(k, land):
        t = lax.rem(j + k, 16)
        return remote(s.m_one.at[land], s.m_one.at[land], s.spread_s.at[1], s.spread_r.at[1], (i, t))

    def m_start(k, carry):
        m_copy(k, j).start()
        return carry

    lax.fori_loop(1, 16, m_start, 0)

    swaps = [
        (w_gate.at[0, pl.ds(others, HALF), :], s.wv.at[2]),
        (w_up.at[0, pl.ds(others, HALF), :], s.wv.at[3]),
        (w_down.at[0, :, pl.ds(others, HALF)], s.wd.at[1]),
    ]
    for n, (src, dst) in enumerate(swaps):
        remote(src, dst, s.swap_s.at[0], s.swap_r.at[n // 2], sibling).start()

    target = iota((256, 256), 0)
    inside = lax.rem(target, 128)
    wanted = (
        lax.div(lax.rem(inside, 32), 2) * 16
        + lax.div(target, 128) * 8
        + lax.rem(inside, 2) * 4
        + lax.div(inside, 32)
    )
    by_head = ones_where(iota((256, 256), 1) == wanted)
    loaded(s.uvv, 4)
    arrived(s.a_recv.at[0:15], s.spread_r.at[0])
    grouped = dot(by_head, s.a_recv[...].reshape(256, 256)).astype(BF)
    values = []
    for h in range(4):
        low = grouped[32 * h : 32 * h + 32]
        high = grouped[128 + 32 * h : 160 + 32 * h]
        values.append((dot(low, s.uvv[h, :256]) + dot(high, s.uvv[h, 256:])).astype(BF))
    values = jnp.concatenate(values, axis=1)
    loaded(s.wov, 5)
    request = iota((32, 1), 0)

    r_send = (s.ra_send, s.rb_send, s.rc_send, s.rd_send)
    r_recv = (s.ra_recv, s.rb_recv, s.rc_recv, s.rd_recv)
    keeps = lax.div(y, 2) == c

    def r_start(p):
        wide = PIECES[p]

        def step(t, carry):
            core, zz = lax.rem(lax.div(t, 4) + y, 2), lax.rem(z + t, 4)
            n = core * 4 + zz
            part = dot(values, s.wov[n, :, STARTS[p] : STARTS[p] + wide])
            own = hidden[:, pl.ds(pl.multiple_of(n * BLK + STARTS[p], 128), wide)].astype(F32)
            part = part + jnp.where(
                request == 2 * j, own[0:1], jnp.where(request == 2 * j + 1, own[1:2], 0.0)
            )
            part = part.astype(BF)
            for h in range(2):
                r_send[p][2 * n + h] = part[16 * h : 16 * h + 16]
            for turned in range(2):
                h = lax.rem(lax.div(y, 2) + turned, 2)
                mine = (core == c) & (zz == z) & (2 * c + h == y)

                @pl.when(jnp.logical_not(mine))
                def _():
                    device = (x * 2 + core, zz * 4 + 2 * c + h)
                    remote(r_send[p].at[2 * n + h], r_recv[p].at[j], s.r_s.at[p], s.r_r.at[p], device).start()

                @pl.when(mine)
                def _():
                    r_recv[p][j] = r_send[p][2 * n + h]

            return carry

        lax.fori_loop(0, 8, step, 0)

    for p in range(4):
        r_start(p)

    arrived(s.m_one.at[0:15], s.spread_r.at[1])
    s.m_all[i] = jnp.sum(s.m_one[...], axis=1)

    def n_copy(k, land):
        t = lax.rem(i + k, 8)
        return remote(s.m_all.at[land], s.m_all.at[land], s.spread_s.at[2], s.spread_r.at[2], (t, j))

    def n_start(k, carry):
        n_copy(k, i).start()
        return carry

    lax.fori_loop(1, 8, n_start, 0)

    pieces = (s.xa, s.xb, s.xc, s.xd)

    def r_sum(p):
        @pl.when(keeps)
        def _():
            arrived(r_recv[p].at[0:15], s.r_r.at[p])

        @pl.when(jnp.logical_not(keeps))
        def _():
            arrived(r_recv[p], s.r_r.at[p])

        block = r_recv[p][0].astype(F32)
        for t in range(1, 16):
            block = block + r_recv[p][t].astype(F32)
        pieces[p][z, x, y] = block.astype(BF)

    def view(p, where):
        return pieces[p].at[tuple(where.get(a, slice(None)) for a in ("z", "x", "y"))]

    def g_start(p):
        first, second, _ = GATHER[p]
        ref = pieces[p].at[z, x, y]
        for m in (2, 1, 3, 0):
            for k in (2, 1, 3, 0):
                if m or k:
                    to = dict(at)
                    to[first], to[second] = turn(first, m), turn(second, k)
                    device = (to["x"] * 2 + c, to["z"] * 4 + to["y"])
                    remote(ref, ref, s.g_s.at[p], s.g_r.at[p, (4 - m) % 4], device).start()

    def h_start(p, m):
        first, _, axis = GATHER[p]
        arrived(r_recv[p].at[0 : 4 if m else 3], s.g_r.at[p, m])
        ref = view(p, {first: turn(first, m), axis: at[axis]})
        for k in (2, 1, 3):
            recv = s.h_r.at[p, 4 - k if axis == "z" else m]
            remote(ref, ref, s.h_s.at[p], recv, place(axis, turn(axis, k), c)).start()

    r_sum(0)
    g_start(0)
    r_sum(1)
    g_start(1)
    r_sum(2)
    g_start(2)
    h_start(0, 0)
    h_start(1, 0)
    r_sum(3)
    g_start(3)
    for m in (1, 3, 2):
        h_start(0, m)
        h_start(1, m)
    for m in (0, 1, 3, 2):
        h_start(2, m)
    for m in (0, 1, 3, 2):
        h_start(3, m)

    arrived(s.m_all.at[0:7], s.spread_r.at[2])
    notes = s.m_all[...].reshape(128, 128)
    notes_high = notes.astype(BF)
    notes_low = (notes - notes_high.astype(F32)).astype(BF)
    picked = dot_nt(ones_where(iota((8, 128), 1) == 32 + iota((8, 128), 0)), notes_high).astype(BF)
    picked = dot(picked, ones_where(lax.div(iota((128, 256), 1), 2) == iota((128, 256), 0)))
    home = iota((1, 256), 1)
    home_key = jnp.where(
        picked[0:1] == lax.rem(home, 2).astype(F32),
        256.0 + picked[1:2] * 16.0 + lax.rem(lax.div(home, 2), 16).astype(F32),
        home.astype(F32),
    )

    def arrange(device, slot):
        size = device.shape[0]
        lanes = iota((size, 128), 1)
        found = ones_where(lanes == device)
        found = dot(found, notes_high) + dot(found, notes_low)
        weigh = jnp.sum(jnp.where(lanes == slot * 16 + j, found, 0.0), axis=1, keepdims=True)
        leaving = jnp.sum(jnp.where(lanes == 32, found, 0.0), axis=1, keepdims=True)
        key = jnp.where(
            leaving == slot.astype(F32), 256.0 + device.astype(F32), (2 * device + slot).astype(F32)
        )
        return ones_where(key == home_key), weigh

    t = iota((256, 1), 0)
    for p in range(3):
        coords = {
            REDUCE[p][0]: lax.div(t, 64),
            REDUCE[p][1]: lax.rem(lax.div(t, 16), 4),
            REDUCE[p][2]: lax.rem(lax.div(t, 4), 4),
        }
        device = (coords["x"] * 2 + lax.rem(lax.div(t, 2), 2)) * 16 + coords["z"] * 4 + coords["y"]
        matrix, weigh = arrange(device, lax.rem(t, 2))
        s.perm[p] = matrix
        s.weight[p] = jnp.broadcast_to(weigh, (256, 128))
    t = iota((16, 1), 0)
    chosen, _ = arrange((x * 2 + lax.rem(lax.div(t, 2), 2)) * 16 + j, lax.rem(t, 2))

    loaded(s.wv.at[0:2], 6)
    arrived(s.wv.at[2:4], s.swap_r.at[0])
    s.pre[...] = jnp.zeros((4, 256, 256), F32)
    s.squares[...] = jnp.zeros((256, 128), F32)

    def project(step, carry):
        kk = step + lax.div(step, 2) - 2 * lax.div(step, 3)
        zz = turn("z", kk)
        for p in range(3):
            arrived(pieces[p].at[0, 0:3], s.h_r.at[p, kk])

        @pl.when(kk > 0)
        def _():
            arrived(pieces[3].at[0], s.h_r.at[3, kk])

        squares = s.squares[...]
        for p in range(4):
            rows = pieces[p][zz].reshape(256, PIECES[p]).astype(F32)
            for n in range(PIECES[p] // 128):
                tile = rows[:, 128 * n : 128 * n + 128]
                squares = squares + tile * tile
            width = pl.multiple_of(c * HALF + zz * BLK + STARTS[p], 128)
            s.xg[:, STARTS[p] : STARTS[p] + PIECES[p]] = (
                rows * gain[:, pl.ds(width, PIECES[p])]
            ).astype(BF)
        s.squares[...] = squares
        depth = pl.multiple_of(zz * BLK, 128)
        for m in range(4):
            s.pre[m] = s.pre[m] + dot(s.xg[...], s.wv[m, pl.ds(depth, BLK), :])
        return carry

    lax.fori_loop(0, 4, project, 0)

    remote(s.squares, s.squares_in, s.half_s.at[0], s.half_r.at[0], sibling).start()
    for m in (2, 3, 0, 1):
        t = (m + 2) % 4
        s.pre_send[m] = s.pre[m].astype(BF)
        remote(
            s.pre_send.at[m], s.pre_recv.at[t], s.half_s.at[1], s.half_r.at[1 + t // 2], sibling
        ).start()
    arrived(s.squares_in, s.half_r.at[0])
    square = jnp.sum(s.squares[...] + s.squares_in[...], axis=1, keepdims=True)
    norm = lax.rsqrt(square / D + 1e-06)
    for b in range(2):
        arrived(s.pre_recv.at[2 * b : 2 * b + 2], s.half_r.at[1 + b])
        gate = (s.pre[2 * b] + s.pre_recv[2 * b].astype(F32)) * norm
        up = (s.pre[2 * b + 1] + s.pre_recv[2 * b + 1].astype(F32)) * norm
        s.inner[b] = (gate / (1.0 + jnp.exp(-gate)) * up).astype(BF)
    def c_start(n, p):
        axis = REDUCE[p][0]
        for k in (2, 1, 3):
            src, dst = s.c_send.at[n, turn(axis, k)], s.c_recv.at[n, k - 1]
            remote(src, dst, s.c_s.at[0], s.c_r.at[n], place(axis, turn(axis, k), c)).start()

    def b_start(n, p):
        axis = REDUCE[p][1]
        for k in (2, 1, 3):
            src, dst = s.b_send.at[n, turn(axis, k)], s.b_recv.at[n, k - 1]
            remote(src, dst, s.b_s.at[0], s.b_r.at[n], place(axis, turn(axis, k), c)).start()

    loaded(s.wd.at[0], 7)
    arrived(s.wd.at[1], s.swap_r.at[1])
    for p, q in CHUNKS:
        n = BASE[p] + q
        if q == 0:
            weigh = s.weight[p][:, 0:1]
            for b in range(2):
                s.sorted_in[p, b] = (dot(s.perm[p], s.inner[b]) * weigh).astype(BF)
        cols = slice(256 * n, 256 * n + 256)
        part = dot(s.sorted_in[p, 0], s.wd[0, :, cols]) + dot(s.sorted_in[p, 1], s.wd[1, :, cols])
        s.c_send[n] = part.astype(BF).reshape(4, 64, 256)
        c_start(n, p)

    for p in range(4):
        for zz in range(4):
            begin = zz * BLK + STARTS[p]
            s.resid[:, begin : begin + PIECES[p]] = dot(chosen, pieces[p][zz].reshape(256, PIECES[p]))

    quarter = lax.div(iota((64, 1), 0), 4)

    def d_start(p):
        axis, first, second = REDUCE[p]
        mine = (at[first] * 4 + at[second]) * 2 + c

        def step(m, carry):
            t = lax.rem(mine + m, 32)
            to = {axis: at[axis], first: lax.div(t, 8), second: lax.rem(lax.div(t, 2), 4)}
            device = (to["x"] * 2 + lax.rem(t, 2), to["z"] * 4 + to["y"])
            remote(s.d_send.at[p, t], s.d_recv.at[p, mine], s.d_s.at[p], s.d_r.at[p], device).start()
            return carry

        lax.fori_loop(1, 32, step, 0)
        s.d_recv[p, mine] = s.d_send[p, mine]

    for p, q in CHUNKS:
        n = BASE[p] + q
        axis = REDUCE[p][0]
        arrived(s.c_recv.at[n], s.c_r.at[n])
        part = s.c_send[n, at[axis]].astype(F32)
        for k in range(3):
            part = part + s.c_recv[n, k].astype(F32)
        if q < COUNT[p] - DIRECT:
            s.b_send[n] = part.astype(BF).reshape(4, 16, 256)
            b_start(n, p)
            continue
        stays = jnp.concatenate([s.resid[:, 256 * n : 256 * n + 256]] * 4, axis=0)
        part = part + jnp.where(quarter == at[REDUCE[p][1]] * 4 + at[REDUCE[p][2]], stays, 0.0)
        begin = 256 * (q + DIRECT - COUNT[p])
        for t in range(32):
            s.d_send[p, t, :, begin : begin + 256] = part[2 * t : 2 * t + 2]
        if q == COUNT[p] - 1:
            d_start(p)

    def f_start(p):
        mine = at[REDUCE[p][2]] * 2 + c
        wide = pl.ds(0, (COUNT[p] - DIRECT) * 256)
        for m in range(1, 8):
            t = lax.rem(mine + m, 8)
            src, dst = s.f_send.at[p, t, :, wide], s.f_recv.at[p, mine, :, wide]
            device = place(REDUCE[p][2], lax.div(t, 2), lax.rem(t, 2))
            remote(src, dst, s.f_s.at[p], s.f_r.at[p], device).start()
        s.f_recv[p, mine] = s.f_send[p, mine]

    last = lax.div(iota((16, 1), 0), 4)
    for p, q in CHUNKS:
        if q >= COUNT[p] - DIRECT:
            continue
        n = BASE[p] + q
        arrived(s.b_recv.at[n], s.b_r.at[n])
        part = s.b_send[n, at[REDUCE[p][1]]].astype(F32)
        for k in range(3):
            part = part + s.b_recv[n, k].astype(F32)
        part = part + jnp.where(last == at[REDUCE[p][2]], s.resid[:, 256 * n : 256 * n + 256], 0.0)
        for t in range(8):
            s.f_send[p, t, :, 256 * q : 256 * q + 256] = part[2 * t : 2 * t + 2]
        if q == COUNT[p] - DIRECT - 1:
            f_start(p)
    for p in (2, 0, 1):
        wide = (COUNT[p] - DIRECT) * 256
        arrived(s.f_recv.at[p, 0:7, :, pl.ds(0, wide)], s.f_r.at[p])
        for core in range(2):
            part = s.f_recv[p, core]
            for t in range(1, 4):
                part = part + s.f_recv[p, 2 * t + core]
            begin = core * HALF + BASE[p] * 256
            out[:, begin : begin + wide] = part[:, :wide].astype(BF)
    for p in (2, 0, 1):
        arrived(s.d_recv.at[p, 0:31], s.d_r.at[p])
        for core in range(2):
            part = s.d_recv[p, core]
            for t in range(1, 16):
                part = part + s.d_recv[p, 2 * t + core]
            begin = core * HALF + (BASE[p] + COUNT[p] - DIRECT) * 256
            out[:, begin : begin + 256 * DIRECT] = part.astype(BF)

    sent(s.a_send.at[0:15], s.spread_s.at[0])
    sent(s.m_one.at[0:15], s.spread_s.at[1])
    sent(s.m_all.at[0:7], s.spread_s.at[2])

    for p in range(4):

        @pl.when(keeps)
        def _():
            sent(r_send[p].at[0:15], s.r_s.at[p])

        @pl.when(jnp.logical_not(keeps))
        def _():
            sent(r_send[p], s.r_s.at[p])

    sent(s.wv.at[0:3], s.swap_s.at[0])
    sent(s.squares, s.half_s.at[0])
    sent(s.pre_send, s.half_s.at[1])
    for p in range(3):
        sent(s.f_send.at[p, 0:7, :, pl.ds(0, (COUNT[p] - DIRECT) * 256)], s.f_s.at[p])
        sent(s.d_send.at[p, 0:31], s.d_s.at[p])
    for p in range(4):
        sent(r_recv[p].at[0:15], s.g_s.at[p])
        sent(pieces[p].at[0:3], s.h_s.at[p])
    sent(s.c_send.at[:, 0:3], s.c_s.at[0])
    sent(s.b_send.at[0 : 14 - 3 * DIRECT, 0:3], s.b_s.at[0])


def on_device(
    hidden,
    q_latent,
    q_rope,
    latent_pages,
    rope_pages,
    block_table,
    cache_len,
    move_req,
    move_to,
    routing,
    gate_weight,
    norm_gain,
    w_uv,
    w_out,
    w_gate,
    w_up,
    w_down,
):
    vmem = pl.BlockSpec(memory_space=pltpu.VMEM)
    smem = pl.BlockSpec(memory_space=pltpu.SMEM)
    hbm = pl.BlockSpec(memory_space=pl.ANY)
    return pl.pallas_call(
        layer,
        out_shape=jax.ShapeDtypeStruct((2, D), BF),
        in_specs=[vmem] * 2 + [smem] * 6 + [hbm] * 9,
        out_specs=vmem,
        scratch_shapes=list(SCRATCH.values()),
        compiler_params=pltpu.CompilerParams(
            collective_id=0, has_side_effects=True, vmem_limit_bytes=56 * 1024 * 1024
        ),
        cost_estimate=pl.CostEstimate(flops=4_000_000_000, bytes_accessed=22_000_000, transcendentals=400_000),
    )(
        hidden,
        norm_gain.reshape(1, D),
        block_table,
        cache_len,
        move_req,
        move_to,
        routing,
        gate_weight,
        q_latent,
        q_rope,
        latent_pages,
        rope_pages,
        w_uv,
        w_out,
        w_gate,
        w_up,
        w_down,
    )


def solution(mesh):
    placed = (
        P(("dp", "ep"), None),
        P(("dp", "ep"), None, None),
        P(("dp", "ep"), None, None),
        P(("dp", "ep"), None, None),
        P(("dp", "ep"), None, None),
        P(("dp", "ep"), None),
        P(("dp", "ep")),
        P(("dp", "ep")),
        P(("dp", "ep")),
        P(("dp", "ep"), None),
        P(("dp", "ep"), None),
        P(),
        P("ep", None, None),
        P("ep", None),
        P("ep", None, "dp"),
        P("ep", None, "dp"),
        P("ep", "dp", None),
    )
    return jax.shard_map(
        on_device, mesh=mesh, in_specs=placed, out_specs=P(("dp", "ep"), None), check_vma=False
    )
```

```python
import types

import jax
import jax.numpy as jnp
from jax import lax
from jax.experimental import pallas as pl
from jax.experimental.pallas import tpu as pltpu
from jax.sharding import PartitionSpec as P

MESH = pl.DeviceIdType.MESH
BF = jnp.bfloat16
F32 = jnp.float32

D = 7168
HALF = D // 2
BLK = 896
PIECES = (256, 128, 256, 256)
STARTS = (0, 256, 384, 640)
GATHER = (("z", "y", "x"), ("z", "x", "y"), ("z", "x", "y"), ("x", "y", "z"))
REDUCE = (("x", "y", "z"), ("y", "z", "x"), ("z", "x", "y"))
BASE = (0, 5, 10)
COUNT = (5, 5, 4)
DIRECT = 1
CHUNKS = [(p, q) for q in range(5) for p in range(3) if q < COUNT[p]]

SCRATCH = dict(
    qv=pltpu.VMEM((2, 64, 512), BF),
    qrv=pltpu.VMEM((2, 64, 64), BF),
    pgv=pltpu.VMEM((24, 64, 512), BF),
    rpv=pltpu.VMEM((24, 32, 128), BF),
    uvv=pltpu.VMEM((4, 512, 128), BF),
    wov=pltpu.VMEM((8, 512, BLK), BF),
    wv=pltpu.VMEM((4, HALF, 256), BF),
    wd=pltpu.VMEM((2, 256, HALF), BF),
    scores=pltpu.VMEM((6, 128, 256), F32),
    a_send=pltpu.VMEM((16, 16, 256), BF),
    a_recv=pltpu.VMEM((16, 16, 256), BF),
    ra_send=pltpu.VMEM((16, 16, PIECES[0]), BF),
    rb_send=pltpu.VMEM((16, 16, PIECES[1]), BF),
    rc_send=pltpu.VMEM((16, 16, PIECES[2]), BF),
    rd_send=pltpu.VMEM((16, 16, PIECES[3]), BF),
    ra_recv=pltpu.VMEM((16, 16, PIECES[0]), BF),
    rb_recv=pltpu.VMEM((16, 16, PIECES[1]), BF),
    rc_recv=pltpu.VMEM((16, 16, PIECES[2]), BF),
    rd_recv=pltpu.VMEM((16, 16, PIECES[3]), BF),
    m_one=pltpu.VMEM((16, 8, 128), F32),
    m_all=pltpu.VMEM((8, 16, 128), F32),
    xa=pltpu.VMEM((4, 4, 4, 16, PIECES[0]), BF),
    xb=pltpu.VMEM((4, 4, 4, 16, PIECES[1]), BF),
    xc=pltpu.VMEM((4, 4, 4, 16, PIECES[2]), BF),
    xd=pltpu.VMEM((4, 4, 4, 16, PIECES[3]), BF),
    xg=pltpu.VMEM((256, BLK), BF),
    pre=pltpu.VMEM((4, 256, 256), F32),
    squares=pltpu.VMEM((256, 128), F32),
    squares_in=pltpu.VMEM((256, 128), F32),
    pre_send=pltpu.VMEM((4, 256, 256), BF),
    pre_recv=pltpu.VMEM((4, 256, 256), BF),
    inner=pltpu.VMEM((2, 256, 256), BF),
    sorted_in=pltpu.VMEM((3, 2, 256, 256), BF),
    perm=pltpu.VMEM((3, 256, 256), BF),
    weight=pltpu.VMEM((3, 256, 128), F32),
    resid=pltpu.VMEM((16, HALF), F32),
    c_send=pltpu.VMEM((14, 4, 64, 256), BF),
    c_recv=pltpu.VMEM((14, 3, 64, 256), BF),
    b_send=pltpu.VMEM((14, 4, 16, 256), BF),
    b_recv=pltpu.VMEM((14, 3, 16, 256), BF),
    f_send=pltpu.VMEM((3, 8, 2, 1280), F32),
    f_recv=pltpu.VMEM((3, 8, 2, 1280), F32),
    d_send=pltpu.VMEM((3, 32, 2, 256 * DIRECT), F32),
    d_recv=pltpu.VMEM((3, 32, 2, 256 * DIRECT), F32),
    load_sem=pltpu.SemaphoreType.DMA((8,)),
    swap_s=pltpu.SemaphoreType.DMA((1,)),
    swap_r=pltpu.SemaphoreType.DMA((2,)),
    half_s=pltpu.SemaphoreType.DMA((2,)),
    half_r=pltpu.SemaphoreType.DMA((3,)),
    spread_s=pltpu.SemaphoreType.DMA((3,)),
    spread_r=pltpu.SemaphoreType.DMA((3,)),
    r_s=pltpu.SemaphoreType.DMA((4,)),
    r_r=pltpu.SemaphoreType.DMA((4,)),
    g_s=pltpu.SemaphoreType.DMA((4,)),
    g_r=pltpu.SemaphoreType.DMA((4, 4)),
    h_s=pltpu.SemaphoreType.DMA((4,)),
    h_r=pltpu.SemaphoreType.DMA((4, 4)),
    c_s=pltpu.SemaphoreType.DMA((1,)),
    c_r=pltpu.SemaphoreType.DMA((14,)),
    b_s=pltpu.SemaphoreType.DMA((1,)),
    b_r=pltpu.SemaphoreType.DMA((14,)),
    f_s=pltpu.SemaphoreType.DMA((3,)),
    f_r=pltpu.SemaphoreType.DMA((3,)),
    d_s=pltpu.SemaphoreType.DMA((3,)),
    d_r=pltpu.SemaphoreType.DMA((3,)),
)


def iota(shape, dim):
    return lax.broadcasted_iota(jnp.int32, shape, dim)


def ones_where(mask):
    return jnp.where(mask, 1.0, 0.0).astype(BF)


def dot(a, b):
    return jnp.dot(a, b, preferred_element_type=F32)


def dot_nt(a, b):
    return lax.dot_general(a, b, (((1,), (1,)), ((), ())), preferred_element_type=F32)


def layer(
    hidden,
    gain,
    table,
    lens,
    move_req,
    move_to,
    routing,
    gates,
    q_latent,
    q_rope,
    pages,
    ropes,
    w_uv,
    w_out,
    w_gate,
    w_up,
    w_down,
    out,
    *scratch,
):
    s = types.SimpleNamespace(**dict(zip(SCRATCH, scratch)))
    i = lax.axis_index("dp")
    j = lax.axis_index("ep")
    x, c = lax.div(i, 2), lax.rem(i, 2)
    z, y = lax.div(j, 4), lax.rem(j, 4)
    other = 1 - c
    at = {"x": x, "y": y, "z": z}

    def place(axis, value, core):
        if axis == "x":
            return (value * 2 + core, j)
        if axis == "y":
            return (x * 2 + core, z * 4 + value)
        return (x * 2 + core, value * 4 + y)

    def turn(axis, k):
        return lax.rem(at[axis] + k, 4)

    def remote(src, dst, send, recv, device):
        return pltpu.make_async_remote_copy(
            src_ref=src, dst_ref=dst, send_sem=send, recv_sem=recv, device_id=device, device_id_type=MESH
        )

    sibling = (x * 2 + other, j)

    def loaded(ref, n):
        pltpu.make_async_copy(ref, ref, s.load_sem.at[n]).wait()

    def arrived(ref, sem):
        remote(ref, ref, sem, sem, sibling).wait_recv()

    def sent(ref, sem):
        remote(ref, ref, sem, sem, sibling).wait_send()

    half = pl.multiple_of(c * HALF, 128)
    others = pl.multiple_of(other * HALF, 128)

    def load(src, dst, n):
        pltpu.make_async_copy(src, dst, s.load_sem.at[n]).start()

    load(q_latent, s.qv, 0)
    load(q_rope, s.qrv, 1)
    load(ropes, s.rpv, 2)
    load(pages, s.pgv, 3)

    barrier = pltpu.get_barrier_semaphore()

    def greet(m, carry):
        t = lax.rem(c * 16 + j + m, 32)
        pl.semaphore_signal(
            barrier, inc=1, device_id=(x * 2 + lax.div(t, 16), lax.rem(t, 16)), device_id_type=MESH
        )
        return carry

    lax.fori_loop(1, 32, greet, 0)
    for k in (1, 2, 3):
        for core in (0, 1):
            pl.semaphore_signal(barrier, inc=1, device_id=place("x", turn("x", k), core), device_id_type=MESH)
        for m in (1, 2, 3):
            for core in (0, 1):
                chip = turn("x", k) * 2 + core
                pl.semaphore_signal(barrier, inc=1, device_id=(chip, turn("z", m) * 4 + y), device_id_type=MESH)
                pl.semaphore_signal(barrier, inc=1, device_id=(chip, z * 4 + turn("y", m)), device_id_type=MESH)

    row = iota((128, 128), 0)
    col = iota((128, 128), 1)
    wanted = lax.rem(lax.div(row, 4), 2) * 64 + lax.div(row, 8) * 4 + lax.rem(row, 4)
    order = ones_where(col == wanted)
    twice = ones_where(iota((64, 128), 0) == lax.rem(iota((64, 128), 1), 64))
    first_row = lax.rem(lax.div(iota((128, 1), 0), 4), 2) == 0
    spread = ones_where(lax.div(iota((256, 128), 0), 2) == iota((256, 128), 1))
    parity = lax.div(iota((256, 128), 1), 64) == lax.rem(iota((256, 128), 0), 2)
    place_of = iota((1, 1536), 1)
    bias = []
    for r in range(2):
        live = jnp.zeros((1, 1536), jnp.int32)
        for q in range(12):
            start = table[r, q] * 64
            count = jnp.clip(lens[r] - q * 64, 0, 64)
            live = jnp.where((place_of >= start) & (place_of < start + count), 1, live)
        bias.append(jnp.where(live > 0, 0.0, -1e30))
    scale = 192.0 ** (-0.5)
    loaded(s.qv, 0)
    loaded(s.qrv, 1)
    query = dot(order, s.qv[...].reshape(128, 512)).astype(BF)
    rotary = dot(dot(order, s.qrv[...].reshape(128, 64)).astype(BF), twice).astype(BF)
    loaded(s.rpv, 2)
    loaded(s.pgv, 3)
    load(w_uv, s.uvv, 4)
    for n in range(8):
        load(w_out.at[:, pl.ds(n * BLK, BLK)], s.wov.at[n], 5)
    load(w_gate.at[0, pl.ds(half, HALF), :], s.wv.at[0], 6)
    load(w_up.at[0, pl.ds(half, HALF), :], s.wv.at[1], 6)
    load(w_down.at[0, :, pl.ds(half, HALF)], s.wd.at[0], 7)
    largest = jnp.full((128, 1), -1e30, F32)
    for n in range(6):
        keys = s.pgv[4 * n : 4 * n + 4].reshape(256, 512)
        turned = dot(spread, s.rpv[4 * n : 4 * n + 4].reshape(128, 128))
        turned = jnp.where(parity, turned, 0.0).astype(BF)
        score = (dot_nt(query, keys) + dot_nt(rotary, turned)) * scale
        cut = slice(256 * n, 256 * n + 256)
        score = score + jnp.where(first_row, bias[0][:, cut], bias[1][:, cut])
        s.scores[n] = score
        largest = jnp.maximum(largest, jnp.max(score, axis=1, keepdims=True))
    total = jnp.zeros((128, 1), F32)
    mixed = jnp.zeros((128, 512), F32)
    for n in range(6):
        prob = jnp.exp(s.scores[n] - largest)
        total = total + jnp.sum(prob, axis=1, keepdims=True)
        mixed = mixed + dot(prob.astype(BF), s.pgv[4 * n : 4 * n + 4].reshape(256, 512))
    mixed = mixed / total
    lower = mixed[:, :256].reshape(16, 8, 256)
    upper = mixed[:, 256:].reshape(16, 8, 256)
    s.a_send[...] = jnp.concatenate([lower, upper], axis=1).astype(BF)
    s.a_recv[j] = s.a_send[j]

    pl.semaphore_wait(barrier, 73)

    def a_copy(k, land):
        t = lax.rem(j + k, 16)
        return remote(s.a_send.at[t], s.a_recv.at[land], s.spread_s.at[0], s.spread_r.at[0], (i, t))

    def a_start(k, carry):
        a_copy(k, j).start()
        return carry

    lax.fori_loop(1, 16, a_start, 0)

    lane = iota((8, 128), 1)
    note = jnp.zeros((8, 128), F32)
    for r in range(2):
        for k in range(8):
            note = jnp.where(lane == routing[r, k] + 16 * r, gates[r, k], note)
    note = jnp.where(lane == 32, move_req[0].astype(F32), note)
    note = jnp.where(lane == 33, move_to[0].astype(F32), note)
    s.m_one[j] = jnp.where(iota((8, 128), 0) == 0, note, 0.0)

    def m_copy(k, land):
        t = lax.rem(j + k, 16)
        return remote(s.m_one.at[land], s.m_one.at[land], s.spread_s.at[1], s.spread_r.at[1], (i, t))

    def m_start(k, carry):
        m_copy(k, j).start()
        return carry

    lax.fori_loop(1, 16, m_start, 0)

    swaps = [
        (w_gate.at[0, pl.ds(others, HALF), :], s.wv.at[2]),
        (w_up.at[0, pl.ds(others, HALF), :], s.wv.at[3]),
        (w_down.at[0, :, pl.ds(others, HALF)], s.wd.at[1]),
    ]
    for n, (src, dst) in enumerate(swaps):
        remote(src, dst, s.swap_s.at[0], s.swap_r.at[n // 2], sibling).start()

    target = iota((256, 256), 0)
    inside = lax.rem(target, 128)
    wanted = (
        lax.div(lax.rem(inside, 32), 2) * 16
        + lax.div(target, 128) * 8
        + lax.rem(inside, 2) * 4
        + lax.div(inside, 32)
    )
    by_head = ones_where(iota((256, 256), 1) == wanted)
    loaded(s.uvv, 4)
    arrived(s.a_recv.at[0:15], s.spread_r.at[0])
    grouped = dot(by_head, s.a_recv[...].reshape(256, 256)).astype(BF)
    values = []
    for h in range(4):
        low = grouped[32 * h : 32 * h + 32]
        high = grouped[128 + 32 * h : 160 + 32 * h]
        values.append((dot(low, s.uvv[h, :256]) + dot(high, s.uvv[h, 256:])).astype(BF))
    values = jnp.concatenate(values, axis=1)
    loaded(s.wov, 5)
    request = iota((32, 1), 0)

    r_send = (s.ra_send, s.rb_send, s.rc_send, s.rd_send)
    r_recv = (s.ra_recv, s.rb_recv, s.rc_recv, s.rd_recv)
    keeps = lax.div(y, 2) == c

    def r_start(p):
        wide = PIECES[p]

        def step(t, carry):
            core, zz = lax.rem(lax.div(t, 4) + y, 2), lax.rem(z + t, 4)
            n = core * 4 + zz
            part = dot(values, s.wov[n, :, STARTS[p] : STARTS[p] + wide])
            own = hidden[:, pl.ds(pl.multiple_of(n * BLK + STARTS[p], 128), wide)].astype(F32)
            part = part + jnp.where(
                request == 2 * j, own[0:1], jnp.where(request == 2 * j + 1, own[1:2], 0.0)
            )
            part = part.astype(BF)
            for h in range(2):
                r_send[p][2 * n + h] = part[16 * h : 16 * h + 16]
            for turned in range(2):
                h = lax.rem(lax.div(y, 2) + turned, 2)
                mine = (core == c) & (zz == z) & (2 * c + h == y)

                @pl.when(jnp.logical_not(mine))
                def _():
                    device = (x * 2 + core, zz * 4 + 2 * c + h)
                    remote(r_send[p].at[2 * n + h], r_recv[p].at[j], s.r_s.at[p], s.r_r.at[p], device).start()

                @pl.when(mine)
                def _():
                    r_recv[p][j] = r_send[p][2 * n + h]

            return carry

        lax.fori_loop(0, 8, step, 0)

    for p in range(4):
        r_start(p)

    arrived(s.m_one.at[0:15], s.spread_r.at[1])
    s.m_all[i] = jnp.sum(s.m_one[...], axis=1)

    def n_copy(k, land):
        t = lax.rem(i + k, 8)
        return remote(s.m_all.at[land], s.m_all.at[land], s.spread_s.at[2], s.spread_r.at[2], (t, j))

    def n_start(k, carry):
        n_copy(k, i).start()
        return carry

    lax.fori_loop(1, 8, n_start, 0)

    pieces = (s.xa, s.xb, s.xc, s.xd)

    def r_sum(p):
        @pl.when(keeps)
        def _():
            arrived(r_recv[p].at[0:15], s.r_r.at[p])

        @pl.when(jnp.logical_not(keeps))
        def _():
            arrived(r_recv[p], s.r_r.at[p])

        block = r_recv[p][0].astype(F32)
        for t in range(1, 16):
            block = block + r_recv[p][t].astype(F32)
        pieces[p][z, x, y] = block.astype(BF)

    def view(p, where):
        return pieces[p].at[tuple(where.get(a, slice(None)) for a in ("z", "x", "y"))]

    def g_start(p):
        first, second, _ = GATHER[p]
        ref = pieces[p].at[z, x, y]
        for m in (2, 1, 3, 0):
            for k in (2, 1, 3, 0):
                if m or k:
                    to = dict(at)
                    to[first], to[second] = turn(first, m), turn(second, k)
                    device = (to["x"] * 2 + c, to["z"] * 4 + to["y"])
                    remote(ref, ref, s.g_s.at[p], s.g_r.at[p, (4 - m) % 4], device).start()

    def h_start(p, m):
        first, _, axis = GATHER[p]
        arrived(r_recv[p].at[0 : 4 if m else 3], s.g_r.at[p, m])
        ref = view(p, {first: turn(first, m), axis: at[axis]})
        for k in (2, 1, 3):
            recv = s.h_r.at[p, 4 - k if axis == "z" else m]
            remote(ref, ref, s.h_s.at[p], recv, place(axis, turn(axis, k), c)).start()

    for p in range(4):
        r_sum(p)
        g_start(p)
    for p, m in ((0, 0), (1, 0), (0, 1), (1, 1), (0, 3), (1, 3), (2, 0), (0, 2), (1, 2), (2, 1), (2, 3), (3, 0)):
        h_start(p, m)
    for p, m in ((2, 2), (3, 1), (3, 3), (3, 2)):
        h_start(p, m)

    arrived(s.m_all.at[0:7], s.spread_r.at[2])
    notes = s.m_all[...].reshape(128, 128)
    notes_high = notes.astype(BF)
    notes_low = (notes - notes_high.astype(F32)).astype(BF)
    picked = dot_nt(ones_where(iota((8, 128), 1) == 32 + iota((8, 128), 0)), notes_high).astype(BF)
    picked = dot(picked, ones_where(lax.div(iota((128, 256), 1), 2) == iota((128, 256), 0)))
    home = iota((1, 256), 1)
    home_key = jnp.where(
        picked[0:1] == lax.rem(home, 2).astype(F32),
        256.0 + picked[1:2] * 16.0 + lax.rem(lax.div(home, 2), 16).astype(F32),
        home.astype(F32),
    )

    def arrange(device, slot):
        size = device.shape[0]
        lanes = iota((size, 128), 1)
        found = ones_where(lanes == device)
        found = dot(found, notes_high) + dot(found, notes_low)
        weigh = jnp.sum(jnp.where(lanes == slot * 16 + j, found, 0.0), axis=1, keepdims=True)
        leaving = jnp.sum(jnp.where(lanes == 32, found, 0.0), axis=1, keepdims=True)
        key = jnp.where(
            leaving == slot.astype(F32), 256.0 + device.astype(F32), (2 * device + slot).astype(F32)
        )
        return ones_where(key == home_key), weigh

    t = iota((256, 1), 0)
    for p in range(3):
        coords = {
            REDUCE[p][0]: lax.div(t, 64),
            REDUCE[p][1]: lax.rem(lax.div(t, 16), 4),
            REDUCE[p][2]: lax.rem(lax.div(t, 4), 4),
        }
        device = (coords["x"] * 2 + lax.rem(lax.div(t, 2), 2)) * 16 + coords["z"] * 4 + coords["y"]
        matrix, weigh = arrange(device, lax.rem(t, 2))
        s.perm[p] = matrix
        s.weight[p] = jnp.broadcast_to(weigh, (256, 128))
    t = iota((16, 1), 0)
    chosen, _ = arrange((x * 2 + lax.rem(lax.div(t, 2), 2)) * 16 + j, lax.rem(t, 2))

    loaded(s.wv.at[0:2], 6)
    arrived(s.wv.at[2:4], s.swap_r.at[0])
    s.pre[...] = jnp.zeros((4, 256, 256), F32)
    s.squares[...] = jnp.zeros((256, 128), F32)

    def project(step, carry):
        kk = step + lax.div(step, 2) - 2 * lax.div(step, 3)
        zz = turn("z", kk)
        for p in range(3):
            arrived(pieces[p].at[0, 0:3], s.h_r.at[p, kk])

        @pl.when(kk > 0)
        def _():
            arrived(pieces[3].at[0], s.h_r.at[3, kk])

        squares = s.squares[...]
        for p in range(4):
            rows = pieces[p][zz].reshape(256, PIECES[p]).astype(F32)
            for n in range(PIECES[p] // 128):
                tile = rows[:, 128 * n : 128 * n + 128]
                squares = squares + tile * tile
            width = pl.multiple_of(c * HALF + zz * BLK + STARTS[p], 128)
            s.xg[:, STARTS[p] : STARTS[p] + PIECES[p]] = (
                rows * gain[:, pl.ds(width, PIECES[p])]
            ).astype(BF)
        s.squares[...] = squares
        depth = pl.multiple_of(zz * BLK, 128)
        for m in range(4):
            s.pre[m] = s.pre[m] + dot(s.xg[...], s.wv[m, pl.ds(depth, BLK), :])
        return carry

    lax.fori_loop(0, 4, project, 0)

    remote(s.squares, s.squares_in, s.half_s.at[0], s.half_r.at[0], sibling).start()
    for m in (2, 3, 0, 1):
        t = (m + 2) % 4
        s.pre_send[m] = s.pre[m].astype(BF)
        remote(
            s.pre_send.at[m], s.pre_recv.at[t], s.half_s.at[1], s.half_r.at[1 + t // 2], sibling
        ).start()
    arrived(s.squares_in, s.half_r.at[0])
    square = jnp.sum(s.squares[...] + s.squares_in[...], axis=1, keepdims=True)
    norm = lax.rsqrt(square / D + 1e-06)
    for b in range(2):
        arrived(s.pre_recv.at[2 * b : 2 * b + 2], s.half_r.at[1 + b])
        gate = (s.pre[2 * b] + s.pre_recv[2 * b].astype(F32)) * norm
        up = (s.pre[2 * b + 1] + s.pre_recv[2 * b + 1].astype(F32)) * norm
        s.inner[b] = (gate / (1.0 + jnp.exp(-gate)) * up).astype(BF)
    def c_start(n, p):
        axis = REDUCE[p][0]
        for k in (2, 1, 3):
            src, dst = s.c_send.at[n, turn(axis, k)], s.c_recv.at[n, k - 1]
            remote(src, dst, s.c_s.at[0], s.c_r.at[n], place(axis, turn(axis, k), c)).start()

    def b_start(n, p):
        axis = REDUCE[p][1]
        for k in (2, 1, 3):
            src, dst = s.b_send.at[n, turn(axis, k)], s.b_recv.at[n, k - 1]
            remote(src, dst, s.b_s.at[0], s.b_r.at[n], place(axis, turn(axis, k), c)).start()

    loaded(s.wd.at[0], 7)
    arrived(s.wd.at[1], s.swap_r.at[1])
    for p, q in CHUNKS:
        n = BASE[p] + q
        if q == 0:
            weigh = s.weight[p][:, 0:1]
            for b in range(2):
                s.sorted_in[p, b] = (dot(s.perm[p], s.inner[b]) * weigh).astype(BF)
        cols = slice(256 * n, 256 * n + 256)
        part = dot(s.sorted_in[p, 0], s.wd[0, :, cols]) + dot(s.sorted_in[p, 1], s.wd[1, :, cols])
        s.c_send[n] = part.astype(BF).reshape(4, 64, 256)
        c_start(n, p)

    for p in range(4):
        for zz in range(4):
            begin = zz * BLK + STARTS[p]
            s.resid[:, begin : begin + PIECES[p]] = dot(chosen, pieces[p][zz].reshape(256, PIECES[p]))

    quarter = lax.div(iota((64, 1), 0), 4)

    def d_start(p):
        axis, first, second = REDUCE[p]
        mine = (at[first] * 4 + at[second]) * 2 + c

        def step(m, carry):
            t = lax.rem(mine + m, 32)
            to = {axis: at[axis], first: lax.div(t, 8), second: lax.rem(lax.div(t, 2), 4)}
            device = (to["x"] * 2 + lax.rem(t, 2), to["z"] * 4 + to["y"])
            remote(s.d_send.at[p, t], s.d_recv.at[p, mine], s.d_s.at[p], s.d_r.at[p], device).start()
            return carry

        lax.fori_loop(1, 32, step, 0)
        s.d_recv[p, mine] = s.d_send[p, mine]

    for p, q in CHUNKS:
        n = BASE[p] + q
        axis = REDUCE[p][0]
        arrived(s.c_recv.at[n], s.c_r.at[n])
        part = s.c_send[n, at[axis]].astype(F32)
        for k in range(3):
            part = part + s.c_recv[n, k].astype(F32)
        if q < COUNT[p] - DIRECT:
            s.b_send[n] = part.astype(BF).reshape(4, 16, 256)
            b_start(n, p)
            continue
        stays = jnp.concatenate([s.resid[:, 256 * n : 256 * n + 256]] * 4, axis=0)
        part = part + jnp.where(quarter == at[REDUCE[p][1]] * 4 + at[REDUCE[p][2]], stays, 0.0)
        begin = 256 * (q + DIRECT - COUNT[p])
        for t in range(32):
            s.d_send[p, t, :, begin : begin + 256] = part[2 * t : 2 * t + 2]
        if q == COUNT[p] - 1:
            d_start(p)

    def f_start(p):
        mine = at[REDUCE[p][2]] * 2 + c
        wide = pl.ds(0, (COUNT[p] - DIRECT) * 256)
        for m in range(1, 8):
            t = lax.rem(mine + m, 8)
            src, dst = s.f_send.at[p, t, :, wide], s.f_recv.at[p, mine, :, wide]
            device = place(REDUCE[p][2], lax.div(t, 2), lax.rem(t, 2))
            remote(src, dst, s.f_s.at[p], s.f_r.at[p], device).start()
        s.f_recv[p, mine] = s.f_send[p, mine]

    last = lax.div(iota((16, 1), 0), 4)
    for p, q in CHUNKS:
        if q >= COUNT[p] - DIRECT:
            continue
        n = BASE[p] + q
        arrived(s.b_recv.at[n], s.b_r.at[n])
        part = s.b_send[n, at[REDUCE[p][1]]].astype(F32)
        for k in range(3):
            part = part + s.b_recv[n, k].astype(F32)
        part = part + jnp.where(last == at[REDUCE[p][2]], s.resid[:, 256 * n : 256 * n + 256], 0.0)
        for t in range(8):
            s.f_send[p, t, :, 256 * q : 256 * q + 256] = part[2 * t : 2 * t + 2]
        if q == COUNT[p] - DIRECT - 1:
            f_start(p)
    for p in (2, 0, 1):
        wide = (COUNT[p] - DIRECT) * 256
        arrived(s.f_recv.at[p, 0:7, :, pl.ds(0, wide)], s.f_r.at[p])
        for core in range(2):
            part = s.f_recv[p, core]
            for t in range(1, 4):
                part = part + s.f_recv[p, 2 * t + core]
            begin = core * HALF + BASE[p] * 256
            out[:, begin : begin + wide] = part[:, :wide].astype(BF)
    for p in (2, 0, 1):
        arrived(s.d_recv.at[p, 0:31], s.d_r.at[p])
        for core in range(2):
            part = s.d_recv[p, core]
            for t in range(1, 16):
                part = part + s.d_recv[p, 2 * t + core]
            begin = core * HALF + (BASE[p] + COUNT[p] - DIRECT) * 256
            out[:, begin : begin + 256 * DIRECT] = part.astype(BF)

    sent(s.a_send.at[0:15], s.spread_s.at[0])
    sent(s.m_one.at[0:15], s.spread_s.at[1])
    sent(s.m_all.at[0:7], s.spread_s.at[2])

    for p in range(4):

        @pl.when(keeps)
        def _():
            sent(r_send[p].at[0:15], s.r_s.at[p])

        @pl.when(jnp.logical_not(keeps))
        def _():
            sent(r_send[p], s.r_s.at[p])

    sent(s.wv.at[0:3], s.swap_s.at[0])
    sent(s.squares, s.half_s.at[0])
    sent(s.pre_send, s.half_s.at[1])
    for p in range(3):
        sent(s.f_send.at[p, 0:7, :, pl.ds(0, (COUNT[p] - DIRECT) * 256)], s.f_s.at[p])
        sent(s.d_send.at[p, 0:31], s.d_s.at[p])
    for p in range(4):
        sent(r_recv[p].at[0:15], s.g_s.at[p])
        sent(pieces[p].at[0:3], s.h_s.at[p])
    sent(s.c_send.at[:, 0:3], s.c_s.at[0])
    sent(s.b_send.at[0 : 14 - 3 * DIRECT, 0:3], s.b_s.at[0])


def on_device(
    hidden,
    q_latent,
    q_rope,
    latent_pages,
    rope_pages,
    block_table,
    cache_len,
    move_req,
    move_to,
    routing,
    gate_weight,
    norm_gain,
    w_uv,
    w_out,
    w_gate,
    w_up,
    w_down,
):
    vmem = pl.BlockSpec(memory_space=pltpu.VMEM)
    smem = pl.BlockSpec(memory_space=pltpu.SMEM)
    hbm = pl.BlockSpec(memory_space=pl.ANY)
    return pl.pallas_call(
        layer,
        out_shape=jax.ShapeDtypeStruct((2, D), BF),
        in_specs=[vmem] * 2 + [smem] * 6 + [hbm] * 9,
        out_specs=vmem,
        scratch_shapes=list(SCRATCH.values()),
        compiler_params=pltpu.CompilerParams(
            collective_id=0, has_side_effects=True, vmem_limit_bytes=56 * 1024 * 1024
        ),
        cost_estimate=pl.CostEstimate(flops=4_000_000_000, bytes_accessed=22_000_000, transcendentals=400_000),
    )(
        hidden,
        norm_gain.reshape(1, D),
        block_table,
        cache_len,
        move_req,
        move_to,
        routing,
        gate_weight,
        q_latent,
        q_rope,
        latent_pages,
        rope_pages,
        w_uv,
        w_out,
        w_gate,
        w_up,
        w_down,
    )


def solution(mesh):
    placed = (
        P(("dp", "ep"), None),
        P(("dp", "ep"), None, None),
        P(("dp", "ep"), None, None),
        P(("dp", "ep"), None, None),
        P(("dp", "ep"), None, None),
        P(("dp", "ep"), None),
        P(("dp", "ep")),
        P(("dp", "ep")),
        P(("dp", "ep")),
        P(("dp", "ep"), None),
        P(("dp", "ep"), None),
        P(),
        P("ep", None, None),
        P("ep", None),
        P("ep", None, "dp"),
        P("ep", None, "dp"),
        P("ep", "dp", None),
    )
    return jax.shard_map(
        on_device, mesh=mesh, in_specs=placed, out_specs=P(("dp", "ep"), None), check_vma=False
    )
```

```python
import types

import jax
import jax.numpy as jnp
from jax import lax
from jax.experimental import pallas as pl
from jax.experimental.pallas import tpu as pltpu
from jax.sharding import PartitionSpec as P

MESH = pl.DeviceIdType.MESH
BF = jnp.bfloat16
F32 = jnp.float32

D = 7168
HALF = D // 2
BLK = 896
PIECES = (256, 128, 256, 256)
STARTS = (0, 256, 384, 640)
GATHER = (("z", "y", "x"), ("z", "x", "y"), ("z", "x", "y"), ("x", "y", "z"))
REDUCE = (("x", "y", "z"), ("y", "z", "x"), ("z", "x", "y"))
BASE = (0, 5, 10)
COUNT = (5, 5, 4)
DIRECT = 1
CHUNKS = [(p, q) for q in range(5) for p in range(3) if q < COUNT[p]]

SCRATCH = dict(
    qv=pltpu.VMEM((2, 64, 512), BF),
    qrv=pltpu.VMEM((2, 64, 64), BF),
    pgv=pltpu.VMEM((24, 64, 512), BF),
    rpv=pltpu.VMEM((24, 32, 128), BF),
    uvv=pltpu.VMEM((4, 512, 128), BF),
    wov=pltpu.VMEM((8, 512, BLK), BF),
    wv=pltpu.VMEM((4, HALF, 256), BF),
    wd=pltpu.VMEM((2, 256, HALF), BF),
    scores=pltpu.VMEM((6, 128, 256), F32),
    a_send=pltpu.VMEM((16, 16, 256), BF),
    a_recv=pltpu.VMEM((16, 16, 256), BF),
    ra_send=pltpu.VMEM((16, 16, PIECES[0]), BF),
    rb_send=pltpu.VMEM((16, 16, PIECES[1]), BF),
    rc_send=pltpu.VMEM((16, 16, PIECES[2]), BF),
    rd_send=pltpu.VMEM((16, 16, PIECES[3]), BF),
    ra_recv=pltpu.VMEM((16, 16, PIECES[0]), BF),
    rb_recv=pltpu.VMEM((16, 16, PIECES[1]), BF),
    rc_recv=pltpu.VMEM((16, 16, PIECES[2]), BF),
    rd_recv=pltpu.VMEM((16, 16, PIECES[3]), BF),
    m_one=pltpu.VMEM((16, 8, 128), F32),
    m_all=pltpu.VMEM((8, 16, 128), F32),
    xa=pltpu.VMEM((4, 4, 4, 16, PIECES[0]), BF),
    xb=pltpu.VMEM((4, 4, 4, 16, PIECES[1]), BF),
    xc=pltpu.VMEM((4, 4, 4, 16, PIECES[2]), BF),
    xd=pltpu.VMEM((4, 4, 4, 16, PIECES[3]), BF),
    xg=pltpu.VMEM((256, BLK), BF),
    pre=pltpu.VMEM((4, 256, 256), F32),
    squares=pltpu.VMEM((256, 128), F32),
    squares_in=pltpu.VMEM((256, 128), F32),
    pre_send=pltpu.VMEM((4, 256, 256), BF),
    pre_recv=pltpu.VMEM((4, 256, 256), BF),
    inner=pltpu.VMEM((2, 256, 256), BF),
    sorted_in=pltpu.VMEM((3, 2, 256, 256), BF),
    perm=pltpu.VMEM((3, 256, 256), BF),
    weight=pltpu.VMEM((3, 256, 128), F32),
    resid=pltpu.VMEM((16, HALF), F32),
    c_send=pltpu.VMEM((14, 4, 64, 256), BF),
    c_recv=pltpu.VMEM((14, 3, 64, 256), BF),
    b_send=pltpu.VMEM((14, 4, 16, 256), BF),
    b_recv=pltpu.VMEM((14, 3, 16, 256), BF),
    f_send=pltpu.VMEM((3, 8, 2, 1280), F32),
    f_recv=pltpu.VMEM((3, 8, 2, 1280), F32),
    d_send=pltpu.VMEM((3, 32, 2, 256 * DIRECT), F32),
    d_recv=pltpu.VMEM((3, 32, 2, 256 * DIRECT), F32),
    load_sem=pltpu.SemaphoreType.DMA((8,)),
    swap_s=pltpu.SemaphoreType.DMA((1,)),
    swap_r=pltpu.SemaphoreType.DMA((2,)),
    half_s=pltpu.SemaphoreType.DMA((2,)),
    half_r=pltpu.SemaphoreType.DMA((3,)),
    spread_s=pltpu.SemaphoreType.DMA((3,)),
    spread_r=pltpu.SemaphoreType.DMA((3,)),
    r_s=pltpu.SemaphoreType.DMA((4,)),
    r_r=pltpu.SemaphoreType.DMA((4,)),
    g_s=pltpu.SemaphoreType.DMA((4,)),
    g_r=pltpu.SemaphoreType.DMA((4, 4)),
    h_s=pltpu.SemaphoreType.DMA((4,)),
    h_r=pltpu.SemaphoreType.DMA((4, 4)),
    c_s=pltpu.SemaphoreType.DMA((1,)),
    c_r=pltpu.SemaphoreType.DMA((14,)),
    b_s=pltpu.SemaphoreType.DMA((1,)),
    b_r=pltpu.SemaphoreType.DMA((14,)),
    f_s=pltpu.SemaphoreType.DMA((3,)),
    f_r=pltpu.SemaphoreType.DMA((3,)),
    d_s=pltpu.SemaphoreType.DMA((3,)),
    d_r=pltpu.SemaphoreType.DMA((3,)),
)


def iota(shape, dim):
    return lax.broadcasted_iota(jnp.int32, shape, dim)


def ones_where(mask):
    return jnp.where(mask, 1.0, 0.0).astype(BF)


def dot(a, b):
    return jnp.dot(a, b, preferred_element_type=F32)


def dot_nt(a, b):
    return lax.dot_general(a, b, (((1,), (1,)), ((), ())), preferred_element_type=F32)


def layer(
    hidden,
    gain,
    table,
    lens,
    move_req,
    move_to,
    routing,
    gates,
    q_latent,
    q_rope,
    pages,
    ropes,
    w_uv,
    w_out,
    w_gate,
    w_up,
    w_down,
    out,
    *scratch,
):
    s = types.SimpleNamespace(**dict(zip(SCRATCH, scratch)))
    i = lax.axis_index("dp")
    j = lax.axis_index("ep")
    x, c = lax.div(i, 2), lax.rem(i, 2)
    z, y = lax.div(j, 4), lax.rem(j, 4)
    other = 1 - c
    at = {"x": x, "y": y, "z": z}

    def place(axis, value, core):
        if axis == "x":
            return (value * 2 + core, j)
        if axis == "y":
            return (x * 2 + core, z * 4 + value)
        return (x * 2 + core, value * 4 + y)

    def turn(axis, k):
        return lax.rem(at[axis] + k, 4)

    def remote(src, dst, send, recv, device):
        return pltpu.make_async_remote_copy(
            src_ref=src, dst_ref=dst, send_sem=send, recv_sem=recv, device_id=device, device_id_type=MESH
        )

    sibling = (x * 2 + other, j)

    def loaded(ref, n):
        pltpu.make_async_copy(ref, ref, s.load_sem.at[n]).wait()

    def arrived(ref, sem):
        remote(ref, ref, sem, sem, sibling).wait_recv()

    def sent(ref, sem):
        remote(ref, ref, sem, sem, sibling).wait_send()

    half = pl.multiple_of(c * HALF, 128)
    others = pl.multiple_of(other * HALF, 128)

    def load(src, dst, n):
        pltpu.make_async_copy(src, dst, s.load_sem.at[n]).start()

    load(q_latent, s.qv, 0)
    load(q_rope, s.qrv, 1)
    load(ropes, s.rpv, 2)
    load(pages, s.pgv, 3)

    barrier = pltpu.get_barrier_semaphore()

    for m in range(1, 16):
        pl.semaphore_signal(barrier, inc=1, device_id=(i, lax.rem(j + m, 16)), device_id_type=MESH)
    for m in range(16):
        pl.semaphore_signal(barrier, inc=1, device_id=(x * 2 + other, m), device_id_type=MESH)
    for k in (1, 2, 3):
        for core in (0, 1):
            pl.semaphore_signal(barrier, inc=1, device_id=place("x", turn("x", k), core), device_id_type=MESH)
        for m in (1, 2, 3):
            for core in (0, 1):
                chip = turn("x", k) * 2 + core
                pl.semaphore_signal(barrier, inc=1, device_id=(chip, turn("z", m) * 4 + y), device_id_type=MESH)
                pl.semaphore_signal(barrier, inc=1, device_id=(chip, z * 4 + turn("y", m)), device_id_type=MESH)

    row = iota((128, 128), 0)
    col = iota((128, 128), 1)
    wanted = lax.rem(lax.div(row, 4), 2) * 64 + lax.div(row, 8) * 4 + lax.rem(row, 4)
    order = ones_where(col == wanted)
    twice = ones_where(iota((64, 128), 0) == lax.rem(iota((64, 128), 1), 64))
    first_row = lax.rem(lax.div(iota((128, 1), 0), 4), 2) == 0
    spread = ones_where(lax.div(iota((256, 128), 0), 2) == iota((256, 128), 1))
    parity = lax.div(iota((256, 128), 1), 64) == lax.rem(iota((256, 128), 0), 2)
    place_of = iota((1, 1536), 1)
    bias = []
    for r in range(2):
        live = jnp.zeros((1, 1536), jnp.int32)
        for q in range(12):
            start = table[r, q] * 64
            count = jnp.clip(lens[r] - q * 64, 0, 64)
            live = jnp.where((place_of >= start) & (place_of < start + count), 1, live)
        bias.append(jnp.where(live > 0, 0.0, -1e30))
    scale = 192.0 ** (-0.5)
    loaded(s.qv, 0)
    loaded(s.qrv, 1)
    query = dot(order, s.qv[...].reshape(128, 512)).astype(BF)
    rotary = dot(dot(order, s.qrv[...].reshape(128, 64)).astype(BF), twice).astype(BF)
    loaded(s.rpv, 2)
    loaded(s.pgv, 3)
    load(w_uv, s.uvv, 4)
    for n in range(8):
        load(w_out.at[:, pl.ds(n * BLK, BLK)], s.wov.at[n], 5)
    load(w_gate.at[0, pl.ds(half, HALF), :], s.wv.at[0], 6)
    load(w_up.at[0, pl.ds(half, HALF), :], s.wv.at[1], 6)
    load(w_down.at[0, :, pl.ds(half, HALF)], s.wd.at[0], 7)
    largest = jnp.full((128, 1), -1e30, F32)
    for n in range(6):
        keys = s.pgv[4 * n : 4 * n + 4].reshape(256, 512)
        turned = dot(spread, s.rpv[4 * n : 4 * n + 4].reshape(128, 128))
        turned = jnp.where(parity, turned, 0.0).astype(BF)
        score = (dot_nt(query, keys) + dot_nt(rotary, turned)) * scale
        cut = slice(256 * n, 256 * n + 256)
        score = score + jnp.where(first_row, bias[0][:, cut], bias[1][:, cut])
        s.scores[n] = score
        largest = jnp.maximum(largest, jnp.max(score, axis=1, keepdims=True))
    total = jnp.zeros((128, 1), F32)
    mixed = jnp.zeros((128, 512), F32)
    for n in range(6):
        prob = jnp.exp(s.scores[n] - largest)
        total = total + jnp.sum(prob, axis=1, keepdims=True)
        mixed = mixed + dot(prob.astype(BF), s.pgv[4 * n : 4 * n + 4].reshape(256, 512))
    mixed = mixed / total
    lower = mixed[:, :256].reshape(16, 8, 256)
    upper = mixed[:, 256:].reshape(16, 8, 256)
    s.a_send[...] = jnp.concatenate([lower, upper], axis=1).astype(BF)
    s.a_recv[j] = s.a_send[j]

    pl.semaphore_wait(barrier, 73)

    def a_copy(k, land):
        t = lax.rem(j + k, 16)
        return remote(s.a_send.at[t], s.a_recv.at[land], s.spread_s.at[0], s.spread_r.at[0], (i, t))

    for k in range(1, 16):
        a_copy(k, j).start()

    lane = iota((8, 128), 1)
    note = jnp.zeros((8, 128), F32)
    for r in range(2):
        for k in range(8):
            note = jnp.where(lane == routing[r, k] + 16 * r, gates[r, k], note)
    note = jnp.where(lane == 32, move_req[0].astype(F32), note)
    note = jnp.where(lane == 33, move_to[0].astype(F32), note)
    s.m_one[j] = jnp.where(iota((8, 128), 0) == 0, note, 0.0)

    def m_copy(k, land):
        t = lax.rem(j + k, 16)
        return remote(s.m_one.at[land], s.m_one.at[land], s.spread_s.at[1], s.spread_r.at[1], (i, t))

    def m_start(k, carry):
        m_copy(k, j).start()
        return carry

    lax.fori_loop(1, 16, m_start, 0)

    swaps = [
        (w_gate.at[0, pl.ds(others, HALF), :], s.wv.at[2]),
        (w_up.at[0, pl.ds(others, HALF), :], s.wv.at[3]),
        (w_down.at[0, :, pl.ds(others, HALF)], s.wd.at[1]),
    ]
    for n, (src, dst) in enumerate(swaps):
        remote(src, dst, s.swap_s.at[0], s.swap_r.at[n // 2], sibling).start()

    target = iota((256, 256), 0)
    inside = lax.rem(target, 128)
    wanted = (
        lax.div(lax.rem(inside, 32), 2) * 16
        + lax.div(target, 128) * 8
        + lax.rem(inside, 2) * 4
        + lax.div(inside, 32)
    )
    by_head = ones_where(iota((256, 256), 1) == wanted)
    loaded(s.uvv, 4)
    arrived(s.a_recv.at[0:15], s.spread_r.at[0])
    grouped = dot(by_head, s.a_recv[...].reshape(256, 256)).astype(BF)
    values = []
    for h in range(4):
        low = grouped[32 * h : 32 * h + 32]
        high = grouped[128 + 32 * h : 160 + 32 * h]
        values.append((dot(low, s.uvv[h, :256]) + dot(high, s.uvv[h, 256:])).astype(BF))
    values = jnp.concatenate(values, axis=1)
    loaded(s.wov, 5)
    request = iota((32, 1), 0)

    r_send = (s.ra_send, s.rb_send, s.rc_send, s.rd_send)
    r_recv = (s.ra_recv, s.rb_recv, s.rc_recv, s.rd_recv)
    keeps = lax.div(y, 2) == c

    def r_start(p):
        wide = PIECES[p]

        def step(t, carry):
            core, zz = lax.rem(lax.div(t, 4) + y, 2), lax.rem(z + t, 4)
            n = core * 4 + zz
            part = dot(values, s.wov[n, :, STARTS[p] : STARTS[p] + wide])
            own = hidden[:, pl.ds(pl.multiple_of(n * BLK + STARTS[p], 128), wide)].astype(F32)
            part = part + jnp.where(
                request == 2 * j, own[0:1], jnp.where(request == 2 * j + 1, own[1:2], 0.0)
            )
            part = part.astype(BF)
            for h in range(2):
                r_send[p][2 * n + h] = part[16 * h : 16 * h + 16]
            for turned in range(2):
                h = lax.rem(lax.div(y, 2) + turned, 2)
                mine = (core == c) & (zz == z) & (2 * c + h == y)

                @pl.when(jnp.logical_not(mine))
                def _():
                    device = (x * 2 + core, zz * 4 + 2 * c + h)
                    remote(r_send[p].at[2 * n + h], r_recv[p].at[j], s.r_s.at[p], s.r_r.at[p], device).start()

                @pl.when(mine)
                def _():
                    r_recv[p][j] = r_send[p][2 * n + h]

            return carry

        lax.fori_loop(0, 8, step, 0)

    for p in range(4):
        r_start(p)

    arrived(s.m_one.at[0:15], s.spread_r.at[1])
    s.m_all[i] = jnp.sum(s.m_one[...], axis=1)

    def n_copy(k, land):
        t = lax.rem(i + k, 8)
        return remote(s.m_all.at[land], s.m_all.at[land], s.spread_s.at[2], s.spread_r.at[2], (t, j))

    def n_start(k, carry):
        n_copy(k, i).start()
        return carry

    lax.fori_loop(1, 8, n_start, 0)

    pieces = (s.xa, s.xb, s.xc, s.xd)

    def r_sum(p):
        @pl.when(keeps)
        def _():
            arrived(r_recv[p].at[0:15], s.r_r.at[p])

        @pl.when(jnp.logical_not(keeps))
        def _():
            arrived(r_recv[p], s.r_r.at[p])

        block = r_recv[p][0].astype(F32)
        for t in range(1, 16):
            block = block + r_recv[p][t].astype(F32)
        pieces[p][z, x, y] = block.astype(BF)

    def view(p, where):
        return pieces[p].at[tuple(where.get(a, slice(None)) for a in ("z", "x", "y"))]

    def g_start(p):
        first, second, _ = GATHER[p]
        ref = pieces[p].at[z, x, y]
        for m in (2, 1, 3, 0):
            for k in (2, 1, 3, 0):
                if m or k:
                    to = dict(at)
                    to[first], to[second] = turn(first, m), turn(second, k)
                    device = (to["x"] * 2 + c, to["z"] * 4 + to["y"])
                    remote(ref, ref, s.g_s.at[p], s.g_r.at[p, (4 - m) % 4], device).start()

    def h_start(p, m):
        first, _, axis = GATHER[p]
        arrived(r_recv[p].at[0 : 4 if m else 3], s.g_r.at[p, m])
        ref = view(p, {first: turn(first, m), axis: at[axis]})
        for k in (2, 1, 3):
            recv = s.h_r.at[p, 4 - k if axis == "z" else m]
            remote(ref, ref, s.h_s.at[p], recv, place(axis, turn(axis, k), c)).start()

    for p in range(4):
        r_sum(p)
        g_start(p)
    for p, m in ((0, 0), (1, 0), (0, 1), (1, 1), (0, 3), (1, 3), (2, 0), (0, 2), (1, 2), (2, 1), (2, 3), (3, 0)):
        h_start(p, m)
    for p, m in ((2, 2), (3, 1), (3, 3), (3, 2)):
        h_start(p, m)

    arrived(s.m_all.at[0:7], s.spread_r.at[2])
    notes = s.m_all[...].reshape(128, 128)
    notes_high = notes.astype(BF)
    notes_low = (notes - notes_high.astype(F32)).astype(BF)
    picked = dot_nt(ones_where(iota((8, 128), 1) == 32 + iota((8, 128), 0)), notes_high).astype(BF)
    picked = dot(picked, ones_where(lax.div(iota((128, 256), 1), 2) == iota((128, 256), 0)))
    home = iota((1, 256), 1)
    home_key = jnp.where(
        picked[0:1] == lax.rem(home, 2).astype(F32),
        256.0 + picked[1:2] * 16.0 + lax.rem(lax.div(home, 2), 16).astype(F32),
        home.astype(F32),
    )

    def arrange(device, slot):
        size = device.shape[0]
        lanes = iota((size, 128), 1)
        found = ones_where(lanes == device)
        found = dot(found, notes_high) + dot(found, notes_low)
        weigh = jnp.sum(jnp.where(lanes == slot * 16 + j, found, 0.0), axis=1, keepdims=True)
        leaving = jnp.sum(jnp.where(lanes == 32, found, 0.0), axis=1, keepdims=True)
        key = jnp.where(
            leaving == slot.astype(F32), 256.0 + device.astype(F32), (2 * device + slot).astype(F32)
        )
        return ones_where(key == home_key), weigh

    t = iota((256, 1), 0)
    for p in range(3):
        coords = {
            REDUCE[p][0]: lax.div(t, 64),
            REDUCE[p][1]: lax.rem(lax.div(t, 16), 4),
            REDUCE[p][2]: lax.rem(lax.div(t, 4), 4),
        }
        device = (coords["x"] * 2 + lax.rem(lax.div(t, 2), 2)) * 16 + coords["z"] * 4 + coords["y"]
        matrix, weigh = arrange(device, lax.rem(t, 2))
        s.perm[p] = matrix
        s.weight[p] = jnp.broadcast_to(weigh, (256, 128))
    t = iota((16, 1), 0)
    chosen, _ = arrange((x * 2 + lax.rem(lax.div(t, 2), 2)) * 16 + j, lax.rem(t, 2))

    loaded(s.wv.at[0:2], 6)
    arrived(s.wv.at[2:4], s.swap_r.at[0])
    s.pre[...] = jnp.zeros((4, 256, 256), F32)
    s.squares[...] = jnp.zeros((256, 128), F32)

    def project(step, carry):
        kk = step + lax.div(step, 2) - 2 * lax.div(step, 3)
        zz = turn("z", kk)
        for p in range(3):
            arrived(pieces[p].at[0, 0:3], s.h_r.at[p, kk])

        @pl.when(kk > 0)
        def _():
            arrived(pieces[3].at[0], s.h_r.at[3, kk])

        squares = s.squares[...]
        for p in range(4):
            rows = pieces[p][zz].reshape(256, PIECES[p]).astype(F32)
            for n in range(PIECES[p] // 128):
                tile = rows[:, 128 * n : 128 * n + 128]
                squares = squares + tile * tile
            width = pl.multiple_of(c * HALF + zz * BLK + STARTS[p], 128)
            s.xg[:, STARTS[p] : STARTS[p] + PIECES[p]] = (
                rows * gain[:, pl.ds(width, PIECES[p])]
            ).astype(BF)
        s.squares[...] = squares
        depth = pl.multiple_of(zz * BLK, 128)
        for m in range(4):
            s.pre[m] = s.pre[m] + dot(s.xg[...], s.wv[m, pl.ds(depth, BLK), :])
        return carry

    lax.fori_loop(0, 4, project, 0)

    remote(s.squares, s.squares_in, s.half_s.at[0], s.half_r.at[0], sibling).start()
    for m in (2, 3, 0, 1):
        t = (m + 2) % 4
        s.pre_send[m] = s.pre[m].astype(BF)
        remote(
            s.pre_send.at[m], s.pre_recv.at[t], s.half_s.at[1], s.half_r.at[1 + t // 2], sibling
        ).start()
    arrived(s.squares_in, s.half_r.at[0])
    square = jnp.sum(s.squares[...] + s.squares_in[...], axis=1, keepdims=True)
    norm = lax.rsqrt(square / D + 1e-06)
    for b in range(2):
        arrived(s.pre_recv.at[2 * b : 2 * b + 2], s.half_r.at[1 + b])
        gate = (s.pre[2 * b] + s.pre_recv[2 * b].astype(F32)) * norm
        up = (s.pre[2 * b + 1] + s.pre_recv[2 * b + 1].astype(F32)) * norm
        s.inner[b] = (gate / (1.0 + jnp.exp(-gate)) * up).astype(BF)
    def c_start(n, p):
        axis = REDUCE[p][0]
        for k in (2, 1, 3):
            src, dst = s.c_send.at[n, turn(axis, k)], s.c_recv.at[n, k - 1]
            remote(src, dst, s.c_s.at[0], s.c_r.at[n], place(axis, turn(axis, k), c)).start()

    def b_start(n, p):
        axis = REDUCE[p][1]
        for k in (2, 1, 3):
            src, dst = s.b_send.at[n, turn(axis, k)], s.b_recv.at[n, k - 1]
            remote(src, dst, s.b_s.at[0], s.b_r.at[n], place(axis, turn(axis, k), c)).start()

    loaded(s.wd.at[0], 7)
    arrived(s.wd.at[1], s.swap_r.at[1])
    for p, q in CHUNKS:
        n = BASE[p] + q
        if q == 0:
            weigh = s.weight[p][:, 0:1]
            for b in range(2):
                s.sorted_in[p, b] = (dot(s.perm[p], s.inner[b]) * weigh).astype(BF)
        cols = slice(256 * n, 256 * n + 256)
        part = dot(s.sorted_in[p, 0], s.wd[0, :, cols]) + dot(s.sorted_in[p, 1], s.wd[1, :, cols])
        s.c_send[n] = part.astype(BF).reshape(4, 64, 256)
        c_start(n, p)

    for p in range(4):
        for zz in range(4):
            begin = zz * BLK + STARTS[p]
            s.resid[:, begin : begin + PIECES[p]] = dot(chosen, pieces[p][zz].reshape(256, PIECES[p]))

    quarter = lax.div(iota((64, 1), 0), 4)

    def d_start(p):
        axis, first, second = REDUCE[p]
        mine = (at[first] * 4 + at[second]) * 2 + c

        def step(m, carry):
            t = lax.rem(mine + m, 32)
            to = {axis: at[axis], first: lax.div(t, 8), second: lax.rem(lax.div(t, 2), 4)}
            device = (to["x"] * 2 + lax.rem(t, 2), to["z"] * 4 + to["y"])
            remote(s.d_send.at[p, t], s.d_recv.at[p, mine], s.d_s.at[p], s.d_r.at[p], device).start()
            return carry

        lax.fori_loop(1, 32, step, 0)
        s.d_recv[p, mine] = s.d_send[p, mine]

    for p, q in CHUNKS:
        n = BASE[p] + q
        axis = REDUCE[p][0]
        arrived(s.c_recv.at[n], s.c_r.at[n])
        part = s.c_send[n, at[axis]].astype(F32)
        for k in range(3):
            part = part + s.c_recv[n, k].astype(F32)
        if q < COUNT[p] - DIRECT:
            s.b_send[n] = part.astype(BF).reshape(4, 16, 256)
            b_start(n, p)
            continue
        stays = jnp.concatenate([s.resid[:, 256 * n : 256 * n + 256]] * 4, axis=0)
        part = part + jnp.where(quarter == at[REDUCE[p][1]] * 4 + at[REDUCE[p][2]], stays, 0.0)
        begin = 256 * (q + DIRECT - COUNT[p])
        for t in range(32):
            s.d_send[p, t, :, begin : begin + 256] = part[2 * t : 2 * t + 2]
        if q == COUNT[p] - 1:
            d_start(p)

    def f_start(p):
        mine = at[REDUCE[p][2]] * 2 + c
        wide = pl.ds(0, (COUNT[p] - DIRECT) * 256)
        for m in range(1, 8):
            t = lax.rem(mine + m, 8)
            src, dst = s.f_send.at[p, t, :, wide], s.f_recv.at[p, mine, :, wide]
            device = place(REDUCE[p][2], lax.div(t, 2), lax.rem(t, 2))
            remote(src, dst, s.f_s.at[p], s.f_r.at[p], device).start()
        s.f_recv[p, mine] = s.f_send[p, mine]

    last = lax.div(iota((16, 1), 0), 4)
    for p, q in CHUNKS:
        if q >= COUNT[p] - DIRECT:
            continue
        n = BASE[p] + q
        arrived(s.b_recv.at[n], s.b_r.at[n])
        part = s.b_send[n, at[REDUCE[p][1]]].astype(F32)
        for k in range(3):
            part = part + s.b_recv[n, k].astype(F32)
        part = part + jnp.where(last == at[REDUCE[p][2]], s.resid[:, 256 * n : 256 * n + 256], 0.0)
        for t in range(8):
            s.f_send[p, t, :, 256 * q : 256 * q + 256] = part[2 * t : 2 * t + 2]
        if q == COUNT[p] - DIRECT - 1:
            f_start(p)
    for p in (2, 0, 1):
        wide = (COUNT[p] - DIRECT) * 256
        arrived(s.f_recv.at[p, 0:7, :, pl.ds(0, wide)], s.f_r.at[p])
        for core in range(2):
            part = s.f_recv[p, core]
            for t in range(1, 4):
                part = part + s.f_recv[p, 2 * t + core]
            begin = core * HALF + BASE[p] * 256
            out[:, begin : begin + wide] = part[:, :wide].astype(BF)
    for p in (2, 0, 1):
        arrived(s.d_recv.at[p, 0:31], s.d_r.at[p])
        for core in range(2):
            part = s.d_recv[p, core]
            for t in range(1, 16):
                part = part + s.d_recv[p, 2 * t + core]
            begin = core * HALF + (BASE[p] + COUNT[p] - DIRECT) * 256
            out[:, begin : begin + 256 * DIRECT] = part.astype(BF)

    sent(s.a_send.at[0:15], s.spread_s.at[0])
    sent(s.m_one.at[0:15], s.spread_s.at[1])
    sent(s.m_all.at[0:7], s.spread_s.at[2])

    for p in range(4):

        @pl.when(keeps)
        def _():
            sent(r_send[p].at[0:15], s.r_s.at[p])

        @pl.when(jnp.logical_not(keeps))
        def _():
            sent(r_send[p], s.r_s.at[p])

    sent(s.wv.at[0:3], s.swap_s.at[0])
    sent(s.squares, s.half_s.at[0])
    sent(s.pre_send, s.half_s.at[1])
    for p in range(3):
        sent(s.f_send.at[p, 0:7, :, pl.ds(0, (COUNT[p] - DIRECT) * 256)], s.f_s.at[p])
        sent(s.d_send.at[p, 0:31], s.d_s.at[p])
    for p in range(4):
        sent(r_recv[p].at[0:15], s.g_s.at[p])
        sent(pieces[p].at[0:3], s.h_s.at[p])
    sent(s.c_send.at[:, 0:3], s.c_s.at[0])
    sent(s.b_send.at[0 : 14 - 3 * DIRECT, 0:3], s.b_s.at[0])


def on_device(
    hidden,
    q_latent,
    q_rope,
    latent_pages,
    rope_pages,
    block_table,
    cache_len,
    move_req,
    move_to,
    routing,
    gate_weight,
    norm_gain,
    w_uv,
    w_out,
    w_gate,
    w_up,
    w_down,
):
    vmem = pl.BlockSpec(memory_space=pltpu.VMEM)
    smem = pl.BlockSpec(memory_space=pltpu.SMEM)
    hbm = pl.BlockSpec(memory_space=pl.ANY)
    return pl.pallas_call(
        layer,
        out_shape=jax.ShapeDtypeStruct((2, D), BF),
        in_specs=[vmem] * 2 + [smem] * 6 + [hbm] * 9,
        out_specs=vmem,
        scratch_shapes=list(SCRATCH.values()),
        compiler_params=pltpu.CompilerParams(
            collective_id=0, has_side_effects=True, vmem_limit_bytes=56 * 1024 * 1024
        ),
        cost_estimate=pl.CostEstimate(flops=4_000_000_000, bytes_accessed=22_000_000, transcendentals=400_000),
    )(
        hidden,
        norm_gain.reshape(1, D),
        block_table,
        cache_len,
        move_req,
        move_to,
        routing,
        gate_weight,
        q_latent,
        q_rope,
        latent_pages,
        rope_pages,
        w_uv,
        w_out,
        w_gate,
        w_up,
        w_down,
    )


def solution(mesh):
    placed = (
        P(("dp", "ep"), None),
        P(("dp", "ep"), None, None),
        P(("dp", "ep"), None, None),
        P(("dp", "ep"), None, None),
        P(("dp", "ep"), None, None),
        P(("dp", "ep"), None),
        P(("dp", "ep")),
        P(("dp", "ep")),
        P(("dp", "ep")),
        P(("dp", "ep"), None),
        P(("dp", "ep"), None),
        P(),
        P("ep", None, None),
        P("ep", None),
        P("ep", None, "dp"),
        P("ep", None, "dp"),
        P("ep", "dp", None),
    )
    return jax.shard_map(
        on_device, mesh=mesh, in_specs=placed, out_specs=P(("dp", "ep"), None), check_vma=False
    )
```
